256 devices in a mesh: rep: 32 (over x, z), fsdp: 8 (over y, core).
Axes of the slice: x: 4, y: 4, z: 8, core: 2. Of those that a mesh axis runs over, the one named last changes fastest.
Arguments:
- raw_grads: bfloat16 [256, 64, 32768], P(('rep', 'fsdp')), may hold values from -6 to 6
- momentum: float32 [32, 64, 32768], P('rep', None, 'fsdp'), may hold values from -6 to 6
- positions: int32 [512, 32], P('fsdp'), may hold values from 0 to 4095, as said below
Outputs:
- new_momentum: float32 [32, 64, 32768], P('rep', None, 'fsdp')
- update: float32 [64, 32768], P(None, 'fsdp')
The draws below stay inside these ranges and needn't reach their ends.
Inputs may be any that keep to these rules, and one draw needn't show every extreme that they name: Each row holds 32 different positions.
All inputs are finite; a program needn't handle non-finite values.
Results may differ from the reference program's by a relative error of at most 0.0003.
Values sent between devices are 32-bit elements; how exact they have to be, the bound alone decides.
A program may use at most 128 MiB of HBM per device.

```python
import math
import jax
import jax.numpy as jnp
from jax import lax

BLOCK = 64
KEEP = 32
SPANS = 512
REPLICAS = 32
WORKERS = 256
N_REP = 32
N_FSDP = 8


def draw_positions(key, part):
    key = jax.random.fold_in(key, 7)
    cells = BLOCK * BLOCK
    row_keys = jax.random.split(key, SPANS)

    def pick_row(subkey):
        return jax.random.permutation(subkey, cells)[:KEEP]
    general = jax.vmap(pick_row)(row_keys)
    first_key = jax.random.fold_in(key, 11)
    inner = jax.random.permutation(first_key, cells - 2)[:KEEP - 2] + 1
    special = jnp.concatenate([jnp.array([0, cells - 1], jnp.int32), inner.astype(jnp.int32)])
    first_row = jnp.arange(SPANS)[:, None] == 0
    return jnp.where(first_row, special[None, :], general).astype(jnp.int32)


def steps_of(own_key, extent, cuts, least, high):
    level, own = 1.0, jax.random.fold_in(own_key, 6)
    for position, shards_of in cuts:
        steps = jnp.exp(jax.random.uniform(jax.random.fold_in(own, position), (shards_of,), jnp.float32, least / len(cuts), high / len(cuts)))
        level = level * jnp.repeat(steps, extent[position] // shards_of).reshape([-1 if axis == position else 1 for axis in range(len(extent))])
    return level


def normal_values(own_key, dims, width, limit, cuts=(), kind=jnp.bfloat16):
    level = steps_of(own_key, dims, cuts, -0.22, 0.18) if cuts else 1.0
    result = jax.random.normal(own_key, dims, jnp.float32) * width * level
    return jnp.minimum(jnp.maximum(result, -limit), limit).astype(kind)


def setup_inputs(seed: int = 0) -> dict:
    key_list = jax.random.split(jax.random.key(seed), 4)
    return {
        "raw_grads": normal_values(key_list[0], (WORKERS, BLOCK, SPANS * BLOCK), 1.0, 6.0, ((0, 256),)),
        "momentum": normal_values(key_list[1], (REPLICAS, BLOCK, SPANS * BLOCK), 1.0, 6.0, ((0, 32), (2, 8)), jnp.float32),
        "positions": draw_positions(jax.random.fold_in(key_list[3], 71), 0),
    }


def dct_cosines(order):
    frequency = jnp.arange(order, dtype=jnp.float32)[:, None]
    samples = jnp.arange(order, dtype=jnp.float32)[None, :]
    cosines = jnp.cos(math.pi * (samples + 0.5) * frequency / order) * math.sqrt(2.0 / order)
    return jnp.where(frequency == 0, cosines * math.sqrt(0.5), cosines)

def forward(field, cosines):
    order = cosines.shape[0]
    left = jnp.dot(cosines, field, precision=lax.Precision.HIGHEST)
    blocks = left.reshape(order, -1, order)
    right = jnp.einsum('rnc,kc->rnk', blocks, cosines, precision=lax.Precision.HIGHEST)
    return right.reshape(order, -1)

def inverse(spectrum, cosines):
    order = cosines.shape[0]
    left = jnp.dot(cosines.T, spectrum, precision=lax.Precision.HIGHEST)
    blocks = left.reshape(order, -1, order)
    right = jnp.einsum('rnk,kc->rnc', blocks, cosines, precision=lax.Precision.HIGHEST)
    return right.reshape(order, -1)

def flat_places(positions, order):
    count = positions.shape[0]
    span_ids = jnp.arange(count, dtype=jnp.int32)[:, None]
    return positions // order * (count * order) + span_ids * order + positions % order

def reference(raw_grads, momentum, positions):
    cosines = dct_cosines(BLOCK)
    places = flat_places(positions, BLOCK).reshape(-1)

    def one_replica(index):
        start = (index * N_FSDP).astype(jnp.int32)
        group = lax.dynamic_slice_in_dim(raw_grads, start, N_FSDP, 0).astype(jnp.float32)
        grads = lax.optimization_barrier(jnp.sum(group, axis=0)) / N_FSDP
        moved = 0.999 * lax.dynamic_index_in_dim(momentum, index.astype(jnp.int32), 0, keepdims=False) + grads
        spectrum = forward(moved, cosines)
        flat = spectrum.reshape(-1)
        shared = flat[places]
        kept = flat.at[places].set(jnp.float32(0.0)).reshape(spectrum.shape)
        return (inverse(kept, cosines), shared)
    new_momentum, shared = lax.map(one_replica, jnp.arange(N_REP, dtype=jnp.int32))
    total = lax.optimization_barrier(jnp.sum(shared, axis=0))
    sparse = jnp.zeros((BLOCK * SPANS * BLOCK,), jnp.float32).at[places].set(total)
    dense = inverse(sparse.reshape(BLOCK, SPANS * BLOCK), cosines)
    blocks = dense.reshape(BLOCK, SPANS, BLOCK)
    scale = jnp.sqrt(lax.optimization_barrier(jnp.mean(blocks * blocks, axis=(0, 2), keepdims=True)) + 1e-06)
    update = jnp.tanh(blocks / scale).reshape(BLOCK, SPANS * BLOCK)
    return (new_momentum, update)
```

```python
import math

import jax
import jax.numpy as jnp
import ml_dtypes
import numpy as np
from jax import lax
from jax.experimental import pallas as pl
from jax.experimental.pallas import tpu as pltpu
from jax.sharding import PartitionSpec as P

MESH = pl.DeviceIdType.MESH
F32, BF16 = jnp.float32, jnp.bfloat16

BLOCK = 64
KEEP = 32
X, Y, Z, CORES = 4, 4, 8, 2
WIDTH = 4096
PIECES = 8
HALF = PIECES // 2
COLS = WIDTH // PIECES
SPANS = COLS // BLOCK
ROWS = SPANS * KEEP
TILES = PIECES * SPANS * KEEP // (8 * 128)
AHEAD, BEHIND, ACROSS = 1, 3, 2


def dct_tables():
    k = np.arange(BLOCK)[:, None]
    j = np.arange(BLOCK)[None, :]
    cosines = np.cos(np.pi * (j + 0.5) * k / BLOCK) * math.sqrt(2.0 / BLOCK)
    cosines = np.where(k == 0, cosines * math.sqrt(0.5), cosines)
    high = cosines.astype(ml_dtypes.bfloat16)
    low = (cosines - high.astype(np.float64)).astype(ml_dtypes.bfloat16)
    return np.concatenate([high, low], axis=1)


def split(x):
    high = x.astype(BF16)
    return high, (x - high.astype(F32)).astype(BF16)


def lanes(shape):
    return lax.broadcasted_iota(jnp.int32, shape, 1)


def own_lane(piece):
    row = lax.broadcasted_iota(jnp.int32, (ROWS, 128), 0)
    return lanes((ROWS, 128)) == lax.rem(row, KEEP) + KEEP * lax.rem(piece, 4)


def unpack(tile, piece):
    wide = jnp.broadcast_to(tile[:, None, :], (SPANS, KEEP, 128)).reshape(ROWS, 128)
    return jnp.sum(jnp.where(own_lane(piece), wide, 0.0), axis=1, keepdims=True)


def pack(column, piece):
    wide = jnp.where(own_lane(piece), column, 0.0)
    return jnp.sum(wide.reshape(SPANS, KEEP, 128), axis=1)


def kernel(
    raw, mom, pos, cos, out_m, out_u,
    raw_v, mom_v, pos_v, cos_v, xsend, part, ya, yb, yc, base, out_v, upd_v,
    places, left, right, left_t, csend, crecv, xslots, zslots,
    raw_sem, in_sem, x_send_sem, x_recv_sem, y_send_sem, y_recv_sem,
    p_send_sem, p_recv_sem, c_send_sem, c_recv_sem,
    rx_send_sem, rx_recv_sem, rz_send_sem, rz_recv_sem, out_sem,
):
    rep, fs = lax.axis_index("rep"), lax.axis_index("fsdp")
    y, core = fs // CORES, lax.rem(fs, CORES)
    x, z = rep // Z, lax.rem(rep, Z)

    def y_peer(step):
        return (rep, lax.rem(y + step, Y) * CORES + core)

    def x_peer(step):
        return (lax.rem(x + step, X) * Z + z, fs)

    def z_peer(step):
        return (x * Z + lax.rem(z + step, Z), fs)

    sibling = (rep, y * CORES + 1 - core)
    peers = [sibling, y_peer(AHEAD), y_peer(BEHIND)]
    peers += [x_peer(s) for s in range(1, X)] + [z_peer(s) for s in range(1, Z)]
    barrier = pltpu.get_barrier_semaphore()
    for peer in peers:
        pl.semaphore_signal(barrier, inc=1, device_id=peer, device_id_type=MESH)

    def raw_copy(k, slot):
        owner = lax.rem(y + k, Y) * CORES + (core if slot == 0 else 1 - core)
        start = pl.multiple_of(owner * WIDTH, WIDTH)
        return pltpu.make_async_copy(
            raw.at[0, :, pl.ds(start, WIDTH)], raw_v.at[k, slot], raw_sem.at[k, slot])

    order = (ACROSS, BEHIND, AHEAD, 0)
    for k in order:
        raw_copy(k, 1).start()
        raw_copy(k, 0).start()
    pos_copy = pltpu.make_async_copy(pos, pos_v, in_sem.at[0])
    cos_copy = pltpu.make_async_copy(cos, cos_v, in_sem.at[1])
    mom_copy = pltpu.make_async_copy(mom.at[0], mom_v, in_sem.at[2])
    pos_copy.start()
    cos_copy.start()
    mom_copy.start()
    pl.semaphore_wait(barrier, len(peers))

    def columns(piece):
        return pl.ds(pl.multiple_of(piece * COLS, COLS), COLS)

    def x_copy(k, p):
        return pltpu.make_async_remote_copy(
            xsend.at[k, p], part.at[k, p], x_send_sem.at[k, p], x_recv_sem.at[k, p],
            device_id=sibling, device_id_type=MESH)

    def to_sibling(k, p):
        xsend[k, p] = raw_v[k, 1, :, columns(p)].astype(F32)
        x_copy(k, p).start()

    for k in order:
        raw_copy(k, 1).wait()

        @pl.loop(0, HALF)
        def _(i):
            to_sibling(k, i)
            to_sibling(k, HALF + i)

        raw_copy(k, 0).wait()

    def y_copy(stage, way, i, src):
        dst = (ya, yb, yc)[stage]
        return pltpu.make_async_remote_copy(
            src, dst.at[way, i], y_send_sem.at[stage, way, i], y_recv_sem.at[stage, way, i],
            device_id=y_peer((BEHIND, AHEAD)[way]), device_id_type=MESH)

    def add_sibling(k, p):
        x_copy(k, p).wait_recv()
        part[k, p] = part[k, p] + raw_v[k, 0, :, columns(p)].astype(F32)

    def source(stage, way, i):
        if stage == 0:
            return ACROSS, (i, HALF + i)[way]
        if stage == 1:
            return (BEHIND, AHEAD)[way], (HALF + i, i)[way]
        return (BEHIND, AHEAD)[way], (i, HALF + i)[way]

    for stage in range(2):
        @pl.loop(0, HALF)
        def _(i):
            for way in range(2):
                k, p = source(stage, way, i)
                add_sibling(k, p)
                y_copy(stage, way, i, part.at[k, p]).start()

    pos_copy.wait()
    cos_copy.wait()
    for m in range(TILES):
        places[0, m] = jnp.concatenate(
            [pos_v[pl.ds(8 * (4 * m + j), 8), :] for j in range(4)], axis=1).astype(F32)

    def p_copy(way):
        return pltpu.make_async_remote_copy(
            places.at[0], places.at[1 + way], p_send_sem.at[way], p_recv_sem.at[way],
            device_id=y_peer((AHEAD, BEHIND)[way]), device_id_type=MESH)

    for way in range(2):
        p_copy(way).start()

    @pl.loop(0, HALF)
    def _(i):
        for way in range(2):
            add_sibling(*source(2, way, i))

    mom_copy.wait()

    @pl.loop(0, PIECES)
    def _(p):
        x_copy(0, p).wait_recv()
        total = part[0, p] + raw_v[0, 0, :, columns(p)].astype(F32)
        base[p] = 0.999 * mom_v[:, columns(p)] + total * 0.125

    def prepare(who, p, transposed):
        place = unpack(places[who, p // 4], p).astype(jnp.int32)
        column = lanes((ROWS, BLOCK))
        pick_row = jnp.where(column == lax.shift_right_logical(place, 6), 1.0, 0.0)
        pick_col = jnp.where(column == lax.bitwise_and(place, 63), 1.0, 0.0)
        rows = jnp.dot(pick_row.astype(BF16), cos_v[...], preferred_element_type=F32)
        cols = jnp.dot(pick_col.astype(BF16), cos_v[...], preferred_element_type=F32)
        lane = lanes((ROWS, 128))
        turned = pltpu.roll(rows, 64, 1)
        left[who, p, :, 0:128] = jnp.where(lane < 64, rows, turned).astype(BF16)
        left[who, p, :, 128:256] = jnp.where(lane < 64, turned, rows).astype(BF16)
        odd = lax.rem(lax.broadcasted_iota(jnp.int32, (ROWS, 128), 0) // KEEP, 2)
        both = cols + pltpu.roll(cols, 64, 1)
        right[who, p] = jnp.where(lane // 64 == odd, both, 0.0)
        if transposed:
            for q in range(SPANS // 2):
                flat = rows[64 * q:64 * q + 64].T
                high, low = flat[0:64].astype(BF16), flat[64:128].astype(BF16)
                left_t[p, q] = jnp.concatenate([high, high, low, low], axis=1)

    @pl.loop(0, PIECES)
    def _(p):
        prepare(0, p, True)

    def coefficients(field, who, p):
        found = []
        for h in range(2):
            high, low = split(field[:, 256 * h:256 * h + 256])
            spread = jnp.concatenate([high, low, high, low], axis=0)
            t = jnp.dot(left[who, p, 128 * h:128 * h + 128, :], spread, preferred_element_type=F32)
            t = jnp.concatenate([t[0:64, 0:128], t[64:128, 128:256]], axis=0)
            found.append(jnp.sum(t * right[who, p, 128 * h:128 * h + 128, :], axis=1, keepdims=True))
        return jnp.concatenate(found, axis=0)

    xslots[x] = jnp.zeros((TILES, 8, 128), F32)
    csend[...] = jnp.zeros((2, TILES, 8, 128), F32)

    @pl.loop(0, PIECES)
    def _(p):
        xslots[x, p // 4] += pack(coefficients(base[p], 0, p), p)

    for way in range(2):
        p_copy(way).wait_recv()

    @pl.loop(0, PIECES)
    def _(p):
        prepare(1, p, False)
        prepare(2, p, False)

    def add_coefficients(way, k, p):
        csend[way, p // 4] += pack(coefficients(part[k, p], (1, 2)[way], p), p)

    @pl.loop(0, HALF)
    def _(i):
        for way in range(2):
            add_coefficients(way, *source(1, way, i))

    @pl.loop(0, HALF)
    def _(i):
        for way in range(2):
            k, p = source(2, way, i)
            y_copy(0, way, i, ya.at[way, i]).wait_recv()
            part[k, p] = part[k, p] + ya[way, i]
            y_copy(2, way, i, part.at[k, p]).start()
            add_coefficients(way, k, p)

    def c_copy(way):
        return pltpu.make_async_remote_copy(
            csend.at[way], crecv.at[way], c_send_sem.at[way], c_recv_sem.at[way],
            device_id=y_peer((BEHIND, AHEAD)[way]), device_id_type=MESH)

    for way in range(2):
        c_copy(way).start()
    for way in range(2):
        c_copy(way).wait_recv()
    xslots[x] = xslots[x] + (crecv[0] + crecv[1]) * 0.125

    def rx_copy(step):
        return pltpu.make_async_remote_copy(
            xslots.at[x], xslots.at[x], rx_send_sem.at[step - 1], rx_recv_sem.at[step - 1],
            device_id=x_peer(step), device_id_type=MESH)

    def rz_copy(step):
        return pltpu.make_async_remote_copy(
            zslots.at[z], zslots.at[z], rz_send_sem.at[step - 1], rz_recv_sem.at[step - 1],
            device_id=z_peer(step), device_id_type=MESH)

    for step in range(1, X):
        rx_copy(step).start()

    def inverse(p, q, column):
        high, low = split(column * right[0, p, 64 * q:64 * q + 64, :])
        spread = jnp.concatenate([high, low, high, low], axis=0)
        return jnp.dot(left_t[p, q], spread, preferred_element_type=F32)

    @pl.loop(0, PIECES)
    def _(p):
        column = unpack(xslots[x, p // 4], p)
        for q in range(SPANS // 2):
            base[p, :, 128 * q:128 * q + 128] -= inverse(p, q, column[64 * q:64 * q + 64])

    for step in range(1, X):
        rx_copy(step).wait_recv()
    zslots[z] = (xslots[0] + xslots[1]) + (xslots[2] + xslots[3])
    for step in range(1, Z):
        rz_copy(step).start()
    for step in range(1, Z):
        rz_copy(step).wait_recv()
    zslots_sum = zslots[0]
    for s in range(1, Z):
        zslots_sum = zslots_sum + zslots[s]
    crecv[0] = zslots_sum

    @pl.loop(0, PIECES)
    def _(p):
        column = unpack(crecv[0, p // 4], p)
        mean = jnp.sum((column * column).reshape(SPANS, KEEP, 1), axis=1, keepdims=True)
        scale = 1.0 / jnp.sqrt(mean * (1.0 / (BLOCK * BLOCK)) + 1e-06)
        column = column * jnp.broadcast_to(scale, (SPANS, KEEP, 1)).reshape(ROWS, 1)
        for q in range(SPANS // 2):
            upd_v[p, :, 128 * q:128 * q + 128] = jnp.tanh(inverse(p, q, column[64 * q:64 * q + 64]))
        pltpu.make_async_copy(upd_v.at[p], out_u.at[:, columns(p)], out_sem.at[0, p]).start()

    @pl.loop(0, HALF)
    def _(i):
        for way in range(2):
            p = (HALF + i, i)[way]
            y_copy(1, way, i, yb.at[way, i]).wait_recv()
            base[p] += yb[way, i] * 0.125

    @pl.loop(0, HALF)
    def _(i):
        for way in range(2):
            p = (i, HALF + i)[way]
            y_copy(2, way, i, yc.at[way, i]).wait_recv()
            out_v[p] = base[p] + yc[way, i] * 0.125
            pltpu.make_async_copy(out_v.at[p], out_m.at[0, :, columns(p)], out_sem.at[1, p]).start()

    for way in range(2):
        p_copy(way).wait_send()
        c_copy(way).wait_send()
    for step in range(1, X):
        rx_copy(step).wait_send()
    for step in range(1, Z):
        rz_copy(step).wait_send()

    @pl.loop(0, PIECES)
    def _(p):
        for k in range(Y):
            x_copy(k, p).wait_send()

    @pl.loop(0, HALF)
    def _(i):
        for stage in range(3):
            for way in range(2):
                y_copy(stage, way, i, ya.at[way, i]).wait_send()

    @pl.loop(0, PIECES)
    def _(p):
        pltpu.make_async_copy(upd_v.at[p], out_u.at[:, columns(p)], out_sem.at[0, p]).wait()
        pltpu.make_async_copy(out_v.at[p], out_m.at[0, :, columns(p)], out_sem.at[1, p]).wait()


def per_device(raw_grads, momentum, positions):
    piece = (BLOCK, COLS)
    tiles = (TILES, 8, 128)
    dma = pltpu.SemaphoreType.DMA
    return pl.pallas_call(
        kernel,
        out_shape=(
            jax.ShapeDtypeStruct((1, BLOCK, WIDTH), F32),
            jax.ShapeDtypeStruct((BLOCK, WIDTH), F32),
        ),
        in_specs=[pl.BlockSpec(memory_space=pl.ANY)] * 4,
        out_specs=(pl.BlockSpec(memory_space=pl.ANY), pl.BlockSpec(memory_space=pl.ANY)),
        scratch_shapes=[
            pltpu.VMEM((Y, 2, BLOCK, WIDTH), BF16),
            pltpu.VMEM((BLOCK, WIDTH), F32),
            pltpu.VMEM((WIDTH // BLOCK, KEEP), jnp.int32),
            pltpu.VMEM((BLOCK, 2 * BLOCK), BF16),
            pltpu.VMEM((Y, PIECES) + piece, F32),
            pltpu.VMEM((Y, PIECES) + piece, F32),
            pltpu.VMEM((2, HALF) + piece, F32),
            pltpu.VMEM((2, HALF) + piece, F32),
            pltpu.VMEM((2, HALF) + piece, F32),
            pltpu.VMEM((PIECES,) + piece, F32),
            pltpu.VMEM((PIECES,) + piece, F32),
            pltpu.VMEM((PIECES,) + piece, F32),
            pltpu.VMEM((3,) + tiles, F32),
            pltpu.VMEM((3, PIECES, ROWS, 256), BF16),
            pltpu.VMEM((3, PIECES, ROWS, 128), F32),
            pltpu.VMEM((PIECES, SPANS // 2, BLOCK, 256), BF16),
            pltpu.VMEM((2,) + tiles, F32),
            pltpu.VMEM((2,) + tiles, F32),
            pltpu.VMEM((X,) + tiles, F32),
            pltpu.VMEM((Z,) + tiles, F32),
            dma((Y, 2)), dma((3,)),
            dma((Y, PIECES)), dma((Y, PIECES)),
            dma((3, 2, HALF)), dma((3, 2, HALF)),
            dma((2,)), dma((2,)), dma((2,)), dma((2,)),
            dma((X - 1,)), dma((X - 1,)), dma((Z - 1,)), dma((Z - 1,)),
            dma((2, PIECES)),
        ],
        compiler_params=pltpu.CompilerParams(
            collective_id=0, has_side_effects=True, vmem_limit_bytes=48 * 1024 * 1024),
    )(raw_grads, momentum, positions, dct_tables())


def solution(mesh):
    placed = (P(("rep", "fsdp"), None, None), P("rep", None, "fsdp"), P("fsdp", None))
    return jax.shard_map(
        per_device,
        mesh=mesh,
        in_specs=placed,
        out_specs=(P("rep", None, "fsdp"), P(None, "fsdp")),
        check_vma=False,
    )
```

```python
import math

import jax
import jax.numpy as jnp
import ml_dtypes
import numpy as np
from jax import lax
from jax.experimental import pallas as pl
from jax.experimental.pallas import tpu as pltpu
from jax.sharding import PartitionSpec as P

MESH = pl.DeviceIdType.MESH
F32, BF16 = jnp.float32, jnp.bfloat16

BLOCK = 64
KEEP = 32
X, Y, Z, CORES = 4, 4, 8, 2
WIDTH = 4096
PIECES = 8
HALF = PIECES // 2
COLS = WIDTH // PIECES
SPANS = COLS // BLOCK
ROWS = SPANS * KEEP
TILES = PIECES * SPANS * KEEP // (8 * 128)
AHEAD, BEHIND, ACROSS = 1, 3, 2
EARLY = 2


def dct_tables():
    k = np.arange(BLOCK)[:, None]
    j = np.arange(BLOCK)[None, :]
    cosines = np.cos(np.pi * (j + 0.5) * k / BLOCK) * math.sqrt(2.0 / BLOCK)
    cosines = np.where(k == 0, cosines * math.sqrt(0.5), cosines)
    high = cosines.astype(ml_dtypes.bfloat16)
    low = (cosines - high.astype(np.float64)).astype(ml_dtypes.bfloat16)
    return np.concatenate([high, low], axis=1)


def split(x):
    high = x.astype(BF16)
    return high, (x - high.astype(F32)).astype(BF16)


def lanes(shape):
    return lax.broadcasted_iota(jnp.int32, shape, 1)


def own_lane(piece):
    row = lax.broadcasted_iota(jnp.int32, (ROWS, 128), 0)
    return lanes((ROWS, 128)) == lax.rem(row, KEEP) + KEEP * lax.rem(piece, 4)


def unpack(tile, piece):
    wide = jnp.broadcast_to(tile[:, None, :], (SPANS, KEEP, 128)).reshape(ROWS, 128)
    return jnp.sum(jnp.where(own_lane(piece), wide, 0.0), axis=1, keepdims=True)


def pack(column, piece):
    wide = jnp.where(own_lane(piece), column, 0.0)
    return jnp.sum(wide.reshape(SPANS, KEEP, 128), axis=1)


def kernel(
    raw, mom, pos, cos, out_m, out_u,
    raw_v, mom_v, pos_v, cos_v, xsend, part, ya, yb, yc, base,
    places, left, right, left_t, csend, crecv, xslots, zslots, total,
    raw_sem, in_sem, go_sem, x_send_sem, x_recv_sem, y_send_sem, y_recv_sem,
    p_send_sem, p_recv_sem, c_send_sem, c_recv_sem,
    rx_send_sem, rx_recv_sem, rz_send_sem, rz_recv_sem, pair_send_sem, pair_recv_sem,
):
    rep, fs = lax.axis_index("rep"), lax.axis_index("fsdp")
    y, core = fs // CORES, lax.rem(fs, CORES)
    x, z = rep // Z, lax.rem(rep, Z)

    def y_peer(step, of=core):
        return (rep, lax.rem(y + step, Y) * CORES + of)

    def x_peer(step):
        return (lax.rem(x + step, X) * Z + z, fs)

    def z_peer(step):
        return (x * Z + lax.rem(z + step, Z), fs)

    sibling = (rep, y * CORES + 1 - core)

    barrier = pltpu.get_barrier_semaphore()

    def greet(peer):
        pl.semaphore_signal(barrier, inc=1, device_id=peer, device_id_type=MESH)

    greet(y_peer(AHEAD, 1))
    greet(y_peer(BEHIND, 1))

    @pl.when(core == 0)
    def _():
        greet(sibling)
        for step in range(1, X):
            greet(x_peer(step))
        for step in range(1, Z):
            greet(z_peer(step))

    def raw_copy(k, slot):
        owner = lax.rem(y + k, Y) * CORES + (core if slot == 0 else 1 - core)
        start = pl.multiple_of(owner * WIDTH, WIDTH)
        return pltpu.make_async_copy(
            raw.at[0, :, pl.ds(start, WIDTH)], raw_v.at[k, slot], raw_sem.at[k, slot])

    order = (ACROSS, BEHIND, AHEAD, 0)
    raw_copy(ACROSS, 1).start()
    raw_copy(ACROSS, 0).start()
    pos_copy = pltpu.make_async_copy(pos, pos_v, in_sem.at[0])
    cos_copy = pltpu.make_async_copy(cos, cos_v, in_sem.at[1])
    mom_copy = pltpu.make_async_copy(mom.at[0], mom_v, in_sem.at[2])
    pos_copy.start()
    cos_copy.start()
    for k in order[1:]:
        raw_copy(k, 1).start()
        raw_copy(k, 0).start()
    mom_copy.start()

    def columns(piece):
        return pl.ds(pl.multiple_of(piece * COLS, COLS), COLS)

    def x_copy(k, p):
        return pltpu.make_async_remote_copy(
            xsend.at[k, p], part.at[k, p], x_send_sem.at[k, p], x_recv_sem.at[k, p],
            device_id=sibling, device_id_type=MESH)

    def widen(k, p):
        xsend[k, p] = raw_v[k, 1, :, columns(p)].astype(F32)

    raw_copy(ACROSS, 1).wait()

    @pl.loop(0, PIECES)
    def _(p):
        widen(ACROSS, p)

    @pl.when(core == 1)
    def _():
        pl.semaphore_wait(barrier, 5)
        pl.semaphore_signal(go_sem, inc=1, device_id=sibling, device_id_type=MESH)

    @pl.when(core == 0)
    def _():
        pl.semaphore_wait(go_sem, 1)

    @pl.loop(0, HALF)
    def _(i):
        x_copy(ACROSS, i).start()
        x_copy(ACROSS, HALF + i).start()

    pos_copy.wait()
    found = pos_v[...].astype(F32).T
    for m in range(TILES):
        places[0, m] = jnp.concatenate(
            [found[8 * (4 * m + j):8 * (4 * m + j) + 8] for j in range(4)], axis=1)

    def p_copy(way):
        return pltpu.make_async_remote_copy(
            places.at[0], places.at[1 + way], p_send_sem.at[way], p_recv_sem.at[way],
            device_id=y_peer((AHEAD, BEHIND)[way]), device_id_type=MESH)

    for way in range(2):
        p_copy(way).start()

    for k in order[1:]:
        raw_copy(k, 1).wait()

        @pl.loop(0, HALF)
        def _(i):
            for p in (i, HALF + i):
                widen(k, p)
                x_copy(k, p).start()

    def y_copy(stage, way, i, src):
        dst = (ya, yb, yc)[stage]
        return pltpu.make_async_remote_copy(
            src, dst.at[way, i], y_send_sem.at[stage, way, i], y_recv_sem.at[stage, way, i],
            device_id=y_peer((BEHIND, AHEAD)[way]), device_id_type=MESH)

    def add_sibling(k, p):
        x_copy(k, p).wait_recv()
        part[k, p] = part[k, p] + raw_v[k, 0, :, columns(p)].astype(F32)

    def source(stage, way, i):
        if stage == 0:
            return ACROSS, (i, HALF + i)[way]
        if stage == 1:
            return (BEHIND, AHEAD)[way], (HALF + i, i)[way]
        return (BEHIND, AHEAD)[way], (i, HALF + i)[way]

    def prepare(who, p, transposed):
        place = unpack(places[who, p // 4], p).astype(jnp.int32)
        column = lanes((ROWS, BLOCK))
        pick_row = jnp.where(column == lax.shift_right_logical(place, 6), 1.0, 0.0)
        pick_col = jnp.where(column == lax.bitwise_and(place, 63), 1.0, 0.0)
        rows = jnp.dot(pick_row.astype(BF16), cos_v[...], preferred_element_type=F32)
        cols = jnp.dot(pick_col.astype(BF16), cos_v[...], preferred_element_type=F32)
        lane = lanes((ROWS, 128))
        turned = pltpu.roll(rows, 64, 1)
        left[who, p, :, 0:128] = jnp.where(lane < 64, rows, turned).astype(BF16)
        left[who, p, :, 128:256] = jnp.where(lane < 64, turned, rows).astype(BF16)
        odd = lax.rem(lax.broadcasted_iota(jnp.int32, (ROWS, 128), 0) // KEEP, 2)
        both = cols + pltpu.roll(cols, 64, 1)
        right[who, p] = jnp.where(lane // 64 == odd, both, 0.0)
        if transposed:
            for q in range(SPANS // 2):
                flat = rows[64 * q:64 * q + 64].T
                high, low = flat[0:64].astype(BF16), flat[64:128].astype(BF16)
                left_t[p, q] = jnp.concatenate([high, high, low, low], axis=1)

    def coefficients(field, who, p):
        found = []
        for h in range(2):
            high, low = split(field[:, 256 * h:256 * h + 256])
            spread = jnp.concatenate([high, low, high, low], axis=0)
            t = jnp.dot(left[who, p, 128 * h:128 * h + 128, :], spread, preferred_element_type=F32)
            t = jnp.concatenate([t[0:64, 0:128], t[64:128, 128:256]], axis=0)
            found.append(jnp.sum(t * right[who, p, 128 * h:128 * h + 128, :], axis=1, keepdims=True))
        return jnp.concatenate(found, axis=0)

    raw_copy(ACROSS, 0).wait()

    @pl.loop(0, HALF)
    def _(i):
        for way in range(2):
            k, p = source(0, way, i)
            add_sibling(k, p)
            y_copy(0, way, i, part.at[k, p]).start()

    for k in order[1:]:
        raw_copy(k, 0).wait()

    @pl.loop(0, EARLY)
    def _(i):
        for way in range(2):
            k, p = source(1, way, i)
            add_sibling(k, p)
            y_copy(1, way, i, part.at[k, p]).start()

    cos_copy.wait()
    for way in range(2):
        p_copy(way).wait_recv()

    for who in (1, 2):
        @pl.loop(0, PIECES, unroll=4)
        def _(p):
            prepare(who, p, False)

    @pl.loop(EARLY, HALF)
    def _(i):
        for way in range(2):
            add_sibling(*source(1, way, i))

    csend[...] = jnp.zeros((2, TILES, 8, 128), F32)

    def add_coefficients(way, k, p):
        csend[way, p // 4] += pack(coefficients(part[k, p], (1, 2)[way], p), p)

    @pl.loop(0, HALF)
    def _(i):
        for way in range(2):
            add_coefficients(way, *source(1, way, i))

    @pl.loop(0, HALF)
    def _(i):
        for way in range(2):
            add_sibling(*source(2, way, i))

    mom_copy.wait()

    @pl.loop(0, PIECES)
    def _(p):
        x_copy(0, p).wait_recv()
        summed = part[0, p] + raw_v[0, 0, :, columns(p)].astype(F32)
        base[p] = 0.999 * mom_v[:, columns(p)] + summed * 0.125

    @pl.loop(0, PIECES, unroll=2)
    def _(p):
        prepare(0, p, True)

    @pl.loop(0, HALF)
    def _(i):
        for way in range(2):
            k, p = source(2, way, i)
            y_copy(0, way, i, ya.at[way, i]).wait_recv()
            part[k, p] = part[k, p] + ya[way, i]
        for way in range(2):
            add_coefficients(way, *source(2, way, i))

    def c_copy(way):
        return pltpu.make_async_remote_copy(
            csend.at[way], crecv.at[way], c_send_sem.at[way], c_recv_sem.at[way],
            device_id=y_peer((BEHIND, AHEAD)[way]), device_id_type=MESH)

    for way in range(2):
        c_copy(way).start()

    @pl.loop(EARLY, HALF)
    def _(i):
        for way in range(2):
            k, p = source(1, way, i)
            y_copy(1, way, i, part.at[k, p]).start()

    @pl.loop(0, HALF)
    def _(i):
        for way in range(2):
            k, p = source(2, way, i)
            y_copy(2, way, i, part.at[k, p]).start()

    xslots[x, core] = jnp.zeros((TILES, 8, 128), F32)

    @pl.loop(0, PIECES, unroll=2)
    def _(p):
        xslots[x, core, p // 4] += pack(coefficients(base[p], 0, p), p)

    for way in range(2):
        c_copy(way).wait_recv()
    xslots[x, core] = xslots[x, core] + (crecv[0] + crecv[1]) * 0.125

    def pair_copy(back):
        ref = total.at[1] if back else xslots.at[x, 1]
        return pltpu.make_async_remote_copy(
            ref, ref, pair_send_sem.at[back], pair_recv_sem.at[back],
            device_id=sibling, device_id_type=MESH)

    def rx_copy(step):
        return pltpu.make_async_remote_copy(
            xslots.at[x], xslots.at[x], rx_send_sem.at[step - 1], rx_recv_sem.at[step - 1],
            device_id=x_peer(step), device_id_type=MESH)

    def rz_copy(step):
        return pltpu.make_async_remote_copy(
            zslots.at[z], zslots.at[z], rz_send_sem.at[step - 1], rz_recv_sem.at[step - 1],
            device_id=z_peer(step), device_id_type=MESH)

    @pl.when(core == 1)
    def _():
        pair_copy(0).start()

    @pl.when(core == 0)
    def _():
        pl.semaphore_wait(barrier, X - 1 + Z - 1)
        pair_copy(0).wait_recv()
        for step in range(1, X):
            rx_copy(step).start()

    def inverse(p, q, column):
        high, low = split(column * right[0, p, 64 * q:64 * q + 64, :])
        spread = jnp.concatenate([high, low, high, low], axis=0)
        return jnp.dot(left_t[p, q], spread, preferred_element_type=F32)

    @pl.loop(0, PIECES, unroll=4)
    def _(p):
        column = unpack(xslots[x, core, p // 4], p)
        for q in range(SPANS // 2):
            base[p, :, 128 * q:128 * q + 128] -= inverse(p, q, column[64 * q:64 * q + 64])

    @pl.when(core == 0)
    def _():
        for step in range(1, X):
            rx_copy(step).wait_recv()
        zslots[z] = (xslots[0] + xslots[1]) + (xslots[2] + xslots[3])
        for step in range(1, Z):
            rz_copy(step).start()
        for step in range(1, Z):
            rz_copy(step).wait_recv()
        summed = zslots[0]
        for s in range(1, Z):
            summed = summed + zslots[s]
        total[...] = summed
        pair_copy(1).start()

    @pl.when(core == 1)
    def _():
        pair_copy(1).wait_recv()

    @pl.loop(0, PIECES, unroll=4)
    def _(p):
        column = unpack(total[core, p // 4], p)
        mean = jnp.sum((column * column).reshape(SPANS, KEEP, 1), axis=1, keepdims=True)
        scale = 1.0 / jnp.sqrt(mean * (1.0 / (BLOCK * BLOCK)) + 1e-06)
        column = column * jnp.broadcast_to(scale, (SPANS, KEEP, 1)).reshape(ROWS, 1)
        for q in range(SPANS // 2):
            at = pl.ds(pl.multiple_of(p * COLS + 128 * q, 128), 128)
            out_u[:, at] = jnp.tanh(inverse(p, q, column[64 * q:64 * q + 64]))

    @pl.loop(0, HALF)
    def _(i):
        for way in range(2):
            p = (HALF + i, i)[way]
            y_copy(1, way, i, yb.at[way, i]).wait_recv()
            base[p] += yb[way, i] * 0.125

    @pl.loop(0, HALF)
    def _(i):
        for way in range(2):
            p = (i, HALF + i)[way]
            y_copy(2, way, i, yc.at[way, i]).wait_recv()
            out_m[0, :, columns(p)] = base[p] + yc[way, i] * 0.125

    for way in range(2):
        p_copy(way).wait_send()
        c_copy(way).wait_send()

    @pl.when(core == 1)
    def _():
        pair_copy(0).wait_send()

    @pl.when(core == 0)
    def _():
        pair_copy(1).wait_send()
        for step in range(1, X):
            rx_copy(step).wait_send()
        for step in range(1, Z):
            rz_copy(step).wait_send()

    @pl.loop(0, PIECES)
    def _(p):
        for k in range(Y):
            x_copy(k, p).wait_send()

    @pl.loop(0, HALF)
    def _(i):
        for stage in range(3):
            for way in range(2):
                y_copy(stage, way, i, ya.at[way, i]).wait_send()


def write_out(new_m, new_u, out_m, out_u, sem):
    copy_m = pltpu.make_async_copy(new_m, out_m, sem.at[0])
    copy_u = pltpu.make_async_copy(new_u, out_u, sem.at[1])
    copy_m.start()
    copy_u.start()
    copy_m.wait()
    copy_u.wait()


def per_device(raw_grads, momentum, positions):
    piece = (BLOCK, COLS)
    tiles = (TILES, 8, 128)
    dma = pltpu.SemaphoreType.DMA
    shapes = ((1, BLOCK, WIDTH), (BLOCK, WIDTH))
    anywhere = pl.BlockSpec(memory_space=pl.ANY)
    inputs = (raw_grads, momentum, positions.T, jnp.asarray(dct_tables()))
    results = pl.pallas_call(
        kernel,
        out_shape=tuple(pltpu.VMEM(shape, F32) for shape in shapes),
        in_specs=[anywhere] * 4,
        out_specs=tuple(pl.BlockSpec(memory_space=pltpu.VMEM) for _ in shapes),
        scratch_shapes=[
            pltpu.VMEM((Y, 2, BLOCK, WIDTH), BF16),
            pltpu.VMEM((BLOCK, WIDTH), F32),
            pltpu.VMEM((KEEP, WIDTH // BLOCK), jnp.int32),
            pltpu.VMEM((BLOCK, 2 * BLOCK), BF16),
            pltpu.VMEM((Y, PIECES) + piece, F32),
            pltpu.VMEM((Y, PIECES) + piece, F32),
            pltpu.VMEM((2, HALF) + piece, F32),
            pltpu.VMEM((2, HALF) + piece, F32),
            pltpu.VMEM((2, HALF) + piece, F32),
            pltpu.VMEM((PIECES,) + piece, F32),
            pltpu.VMEM((3,) + tiles, F32),
            pltpu.VMEM((3, PIECES, ROWS, 256), BF16),
            pltpu.VMEM((3, PIECES, ROWS, 128), F32),
            pltpu.VMEM((PIECES, SPANS // 2, BLOCK, 256), BF16),
            pltpu.VMEM((2,) + tiles, F32),
            pltpu.VMEM((2,) + tiles, F32),
            pltpu.VMEM((X, CORES) + tiles, F32),
            pltpu.VMEM((Z, CORES) + tiles, F32),
            pltpu.VMEM((CORES,) + tiles, F32),
            dma((Y, 2)), dma((3,)), pltpu.SemaphoreType.REGULAR,
            dma((Y, PIECES)), dma((Y, PIECES)),
            dma((3, 2, HALF)), dma((3, 2, HALF)),
            dma((2,)), dma((2,)), dma((2,)), dma((2,)),
            dma((X - 1,)), dma((X - 1,)), dma((Z - 1,)), dma((Z - 1,)),
            dma((2,)), dma((2,)),
        ],
        compiler_params=pltpu.CompilerParams(
            collective_id=0, has_side_effects=True, vmem_limit_bytes=48 * 1024 * 1024),
    )(*(pltpu.with_memory_space_constraint(v, pltpu.HBM) for v in inputs))
    return pl.pallas_call(
        write_out,
        out_shape=tuple(pltpu.HBM(shape, F32) for shape in shapes),
        in_specs=[anywhere] * 2,
        out_specs=(anywhere, anywhere),
        scratch_shapes=[dma((2,))],
        compiler_params=pltpu.CompilerParams(vmem_limit_bytes=4 * 1024 * 1024),
    )(*(pltpu.with_memory_space_constraint(v, pltpu.VMEM) for v in results))


def solution(mesh):
    placed = (P(("rep", "fsdp"), None, None), P("rep", None, "fsdp"), P("fsdp", None))
    return jax.shard_map(
        per_device,
        mesh=mesh,
        in_specs=placed,
        out_specs=(P("rep", None, "fsdp"), P(None, "fsdp")),
        check_vma=False,
    )
```

```python
import math

import jax
import jax.numpy as jnp
import ml_dtypes
import numpy as np
from jax import lax
from jax.experimental import pallas as pl
from jax.experimental.pallas import tpu as pltpu
from jax.sharding import PartitionSpec as P

MESH = pl.DeviceIdType.MESH
F32, BF16 = jnp.float32, jnp.bfloat16

BLOCK = 64
KEEP = 32
X, Y, Z, CORES = 4, 4, 8, 2
WIDTH = 4096
PIECES = 8
HALF = PIECES // 2
COLS = WIDTH // PIECES
SPANS = COLS // BLOCK
ROWS = SPANS * KEEP
TILES = PIECES * SPANS * KEEP // (8 * 128)
AHEAD, BEHIND, ACROSS = 1, 3, 2
X_STEPS, Z_STEPS = (2, 1, 3), (4, 3, 5, 2, 6, 1, 7)
EARLY = 1


def dct_tables():
    k = np.arange(BLOCK)[:, None]
    j = np.arange(BLOCK)[None, :]
    cosines = np.cos(np.pi * (j + 0.5) * k / BLOCK) * math.sqrt(2.0 / BLOCK)
    cosines = np.where(k == 0, cosines * math.sqrt(0.5), cosines)
    high = cosines.astype(ml_dtypes.bfloat16)
    low = (cosines - high.astype(np.float64)).astype(ml_dtypes.bfloat16)
    return np.concatenate([high, low], axis=1)


def split(x):
    high = x.astype(BF16)
    return high, (x - high.astype(F32)).astype(BF16)


def lanes(shape):
    return lax.broadcasted_iota(jnp.int32, shape, 1)


def own_lane(piece):
    row = lax.broadcasted_iota(jnp.int32, (ROWS, 128), 0)
    return lanes((ROWS, 128)) == lax.rem(row, KEEP) + KEEP * lax.rem(piece, 4)


def unpack(tile, piece):
    wide = jnp.broadcast_to(tile[:, None, :], (SPANS, KEEP, 128)).reshape(ROWS, 128)
    return jnp.sum(jnp.where(own_lane(piece), wide, 0.0), axis=1, keepdims=True)


def pack(column, piece):
    wide = jnp.where(own_lane(piece), column, 0.0)
    return jnp.sum(wide.reshape(SPANS, KEEP, 128), axis=1)


def kernel(
    raw, mom, pos, cos, out_m, out_u,
    raw_v, mom_v, pos_v, cos_v, xsend, part, ya, yb, yc, base,
    places, left, right, left_t, csend, crecv, xslots, zslots, total,
    raw_sem, in_sem, go_sem, x_send_sem, x_recv_sem, y_send_sem, y_recv_sem,
    p_send_sem, p_recv_sem, c_send_sem, c_recv_sem,
    rx_send_sem, rx_recv_sem, rz_send_sem, rz_recv_sem, pair_send_sem, pair_recv_sem,
):
    rep, fs = lax.axis_index("rep"), lax.axis_index("fsdp")
    y, core = fs // CORES, lax.rem(fs, CORES)
    x, z = rep // Z, lax.rem(rep, Z)

    def y_peer(step, of=core):
        return (rep, lax.rem(y + step, Y) * CORES + of)

    def x_peer(step):
        return (lax.rem(x + step, X) * Z + z, fs)

    def z_peer(step):
        return (x * Z + lax.rem(z + step, Z), fs)

    sibling = (rep, y * CORES + 1 - core)

    barrier = pltpu.get_barrier_semaphore()

    def greet(peer):
        pl.semaphore_signal(barrier, inc=1, device_id=peer, device_id_type=MESH)

    greet(y_peer(AHEAD, 1))
    greet(y_peer(BEHIND, 1))

    @pl.when(core == 0)
    def _():
        greet(sibling)

    def raw_copy(k, slot):
        owner = lax.rem(y + k, Y) * CORES + (core if slot == 0 else 1 - core)
        start = pl.multiple_of(owner * WIDTH, WIDTH)
        return pltpu.make_async_copy(
            raw.at[0, :, pl.ds(start, WIDTH)], raw_v.at[k, slot], raw_sem.at[k, slot])

    order = (ACROSS, BEHIND, AHEAD, 0)
    pos_copy = pltpu.make_async_copy(pos, pos_v, in_sem.at[0])
    cos_copy = pltpu.make_async_copy(cos, cos_v, in_sem.at[1])
    mom_copy = pltpu.make_async_copy(mom.at[0], mom_v, in_sem.at[2])
    raw_copy(ACROSS, 1).start()
    pos_copy.start()
    raw_copy(ACROSS, 0).start()

    def columns(piece):
        return pl.ds(pl.multiple_of(piece * COLS, COLS), COLS)

    def x_copy(k, p):
        return pltpu.make_async_remote_copy(
            xsend.at[k, p], part.at[k, p], x_send_sem.at[k, p], x_recv_sem.at[k, p],
            device_id=sibling, device_id_type=MESH)

    def widen(k, p):
        xsend[k, p] = raw_v[k, 1, :, columns(p)].astype(F32)

    pos_copy.wait()
    found = pos_v[...].astype(F32).T
    for m in range(TILES):
        places[0, m] = jnp.concatenate(
            [found[8 * (4 * m + j):8 * (4 * m + j) + 8] for j in range(4)], axis=1)

    def p_copy(way):
        return pltpu.make_async_remote_copy(
            places.at[0], places.at[1 + way], p_send_sem.at[way], p_recv_sem.at[way],
            device_id=y_peer((AHEAD, BEHIND)[way]), device_id_type=MESH)

    raw_copy(ACROSS, 1).wait()

    @pl.loop(0, PIECES)
    def _(p):
        widen(ACROSS, p)

    @pl.when(core == 1)
    def _():
        pl.semaphore_wait(barrier, 5)
        pl.semaphore_signal(go_sem, inc=1, device_id=sibling, device_id_type=MESH)

    @pl.when(core == 0)
    def _():
        pl.semaphore_wait(go_sem, 1)

    x_copy(ACROSS, 0).start()
    x_copy(ACROSS, HALF).start()
    for way in range(2):
        p_copy(way).start()

    @pl.loop(1, HALF)
    def _(i):
        x_copy(ACROSS, i).start()
        x_copy(ACROSS, HALF + i).start()

    for k in order[1:]:
        raw_copy(k, 1).start()
        raw_copy(k, 0).start()
    cos_copy.start()
    mom_copy.start()

    def y_copy(stage, way, i, src):
        dst = (ya, yb, yc)[stage]
        return pltpu.make_async_remote_copy(
            src, dst.at[way, i], y_send_sem.at[stage, way, i], y_recv_sem.at[stage, way, i],
            device_id=y_peer((BEHIND, AHEAD)[way]), device_id_type=MESH)

    def add_sibling(k, p):
        x_copy(k, p).wait_recv()
        part[k, p] = part[k, p] + raw_v[k, 0, :, columns(p)].astype(F32)

    def source(stage, way, i):
        if stage == 0:
            return ACROSS, (i, HALF + i)[way]
        if stage == 1:
            return (BEHIND, AHEAD)[way], (HALF + i, i)[way]
        return (BEHIND, AHEAD)[way], (i, HALF + i)[way]

    def prepare(who, p, transposed):
        place = unpack(places[who, p // 4], p).astype(jnp.int32)
        column = lanes((ROWS, BLOCK))
        pick_row = jnp.where(column == lax.shift_right_logical(place, 6), 1.0, 0.0)
        pick_col = jnp.where(column == lax.bitwise_and(place, 63), 1.0, 0.0)
        rows = jnp.dot(pick_row.astype(BF16), cos_v[...], preferred_element_type=F32)
        cols = jnp.dot(pick_col.astype(BF16), cos_v[...], preferred_element_type=F32)
        lane = lanes((ROWS, 128))
        turned = pltpu.roll(rows, 64, 1)
        left[who, p, :, 0:128] = jnp.where(lane < 64, rows, turned).astype(BF16)
        left[who, p, :, 128:256] = jnp.where(lane < 64, turned, rows).astype(BF16)
        odd = lax.rem(lax.broadcasted_iota(jnp.int32, (ROWS, 128), 0) // KEEP, 2)
        both = cols + pltpu.roll(cols, 64, 1)
        right[who, p] = jnp.where(lane // 64 == odd, both, 0.0)
        if transposed:
            for q in range(SPANS // 2):
                flat = rows[64 * q:64 * q + 64].T
                high, low = flat[0:64].astype(BF16), flat[64:128].astype(BF16)
                left_t[p, q] = jnp.concatenate([high, high, low, low], axis=1)

    def coefficients(field, who, p):
        found = []
        for h in range(2):
            high, low = split(field[:, 256 * h:256 * h + 256])
            spread = jnp.concatenate([high, low, high, low], axis=0)
            t = jnp.dot(left[who, p, 128 * h:128 * h + 128, :], spread, preferred_element_type=F32)
            t = jnp.concatenate([t[0:64, 0:128], t[64:128, 128:256]], axis=0)
            found.append(jnp.sum(t * right[who, p, 128 * h:128 * h + 128, :], axis=1, keepdims=True))
        return jnp.concatenate(found, axis=0)

    raw_copy(ACROSS, 0).wait()

    @pl.loop(0, HALF)
    def _(i):
        for way in range(2):
            k, p = source(0, way, i)
            add_sibling(k, p)
            y_copy(0, way, i, part.at[k, p]).start()

    for k in order[1:]:
        raw_copy(k, 1).wait()

        @pl.loop(0, HALF)
        def _(i):
            for p in (i, HALF + i):
                widen(k, p)
                x_copy(k, p).start()

    @pl.when(core == 0)
    def _():
        for step in range(1, X):
            greet(x_peer(step))
        for step in range(1, Z):
            greet(z_peer(step))

    for k in order[1:]:
        raw_copy(k, 0).wait()

    @pl.loop(0, EARLY)
    def _(i):
        for way in range(2):
            k, p = source(1, way, i)
            add_sibling(k, p)
            y_copy(1, way, i, part.at[k, p]).start()

    cos_copy.wait()
    for way in range(2):
        p_copy(way).wait_recv()

    for who in (1, 2):
        @pl.loop(0, PIECES, unroll=4)
        def _(p):
            prepare(who, p, False)

    @pl.loop(EARLY, HALF)
    def _(i):
        for way in range(2):
            add_sibling(*source(1, way, i))

    csend[...] = jnp.zeros((2, TILES, 8, 128), F32)

    def add_coefficients(way, k, p):
        csend[way, p // 4] += pack(coefficients(part[k, p], (1, 2)[way], p), p)

    @pl.loop(0, HALF)
    def _(i):
        for way in range(2):
            add_coefficients(way, *source(1, way, i))

    @pl.loop(0, HALF)
    def _(i):
        for way in range(2):
            add_sibling(*source(2, way, i))

    mom_copy.wait()

    @pl.loop(0, PIECES)
    def _(p):
        x_copy(0, p).wait_recv()
        summed = part[0, p] + raw_v[0, 0, :, columns(p)].astype(F32)
        base[p] = 0.999 * mom_v[:, columns(p)] + summed * 0.125

    @pl.loop(0, PIECES, unroll=2)
    def _(p):
        prepare(0, p, True)

    @pl.loop(0, HALF)
    def _(i):
        for way in range(2):
            k, p = source(2, way, i)
            y_copy(0, way, i, ya.at[way, i]).wait_recv()
            part[k, p] = part[k, p] + ya[way, i]
        for way in range(2):
            add_coefficients(way, *source(2, way, i))

    def c_copy(way):
        return pltpu.make_async_remote_copy(
            csend.at[way], crecv.at[way], c_send_sem.at[way], c_recv_sem.at[way],
            device_id=y_peer((BEHIND, AHEAD)[way]), device_id_type=MESH)

    for way in range(2):
        c_copy(way).start()

    def send_rest():
        @pl.loop(EARLY, HALF)
        def _(i):
            for way in range(2):
                k, p = source(1, way, i)
                y_copy(1, way, i, part.at[k, p]).start()

        @pl.loop(0, HALF)
        def _(i):
            for way in range(2):
                k, p = source(2, way, i)
                y_copy(2, way, i, part.at[k, p]).start()

    pl.when(core == 1)(send_rest)

    xslots[x, core] = jnp.zeros((TILES, 8, 128), F32)

    @pl.loop(0, PIECES, unroll=2)
    def _(p):
        xslots[x, core, p // 4] += pack(coefficients(base[p], 0, p), p)

    for way in range(2):
        c_copy(way).wait_recv()
    xslots[x, core] = xslots[x, core] + (crecv[0] + crecv[1]) * 0.125

    def pair_copy(back):
        ref = total.at[1] if back else xslots.at[x, 1]
        return pltpu.make_async_remote_copy(
            ref, ref, pair_send_sem.at[back], pair_recv_sem.at[back],
            device_id=sibling, device_id_type=MESH)

    def rx_copy(step):
        return pltpu.make_async_remote_copy(
            xslots.at[x], xslots.at[x], rx_send_sem.at[step - 1], rx_recv_sem.at[step - 1],
            device_id=x_peer(step), device_id_type=MESH)

    def rz_copy(step):
        return pltpu.make_async_remote_copy(
            zslots.at[z], zslots.at[z], rz_send_sem.at[step - 1], rz_recv_sem.at[step - 1],
            device_id=z_peer(step), device_id_type=MESH)

    @pl.when(core == 1)
    def _():
        pair_copy(0).start()

    @pl.when(core == 0)
    def _():
        pl.semaphore_wait(barrier, X - 1 + Z - 1)
        pair_copy(0).wait_recv()
        for step in X_STEPS:
            rx_copy(step).start()

    def inverse(p, q, column):
        high, low = split(column * right[0, p, 64 * q:64 * q + 64, :])
        spread = jnp.concatenate([high, low, high, low], axis=0)
        return jnp.dot(left_t[p, q], spread, preferred_element_type=F32)

    @pl.loop(0, PIECES, unroll=4)
    def _(p):
        column = unpack(xslots[x, core, p // 4], p)
        for q in range(SPANS // 2):
            base[p, :, 128 * q:128 * q + 128] -= inverse(p, q, column[64 * q:64 * q + 64])

    @pl.when(core == 0)
    def _():
        for step in range(1, X):
            rx_copy(step).wait_recv()
        send_rest()
        zslots[z] = (xslots[0] + xslots[1]) + (xslots[2] + xslots[3])
        for step in Z_STEPS:
            rz_copy(step).start()
        for step in range(1, Z):
            rz_copy(step).wait_recv()
        summed = zslots[0]
        for s in range(1, Z):
            summed = summed + zslots[s]
        total[...] = summed
        pair_copy(1).start()

    @pl.when(core == 1)
    def _():
        pair_copy(1).wait_recv()

    @pl.loop(0, PIECES, unroll=4)
    def _(p):
        column = unpack(total[core, p // 4], p)
        mean = jnp.sum((column * column).reshape(SPANS, KEEP, 1), axis=1, keepdims=True)
        scale = 1.0 / jnp.sqrt(mean * (1.0 / (BLOCK * BLOCK)) + 1e-06)
        column = column * jnp.broadcast_to(scale, (SPANS, KEEP, 1)).reshape(ROWS, 1)
        for q in range(SPANS // 2):
            at = pl.ds(pl.multiple_of(p * COLS + 128 * q, 128), 128)
            out_u[:, at] = jnp.tanh(inverse(p, q, column[64 * q:64 * q + 64]))

    @pl.loop(0, HALF)
    def _(i):
        for way in range(2):
            p = (HALF + i, i)[way]
            y_copy(1, way, i, yb.at[way, i]).wait_recv()
            base[p] += yb[way, i] * 0.125

    for way in range(2):
        p_copy(way).wait_send()
        c_copy(way).wait_send()

    @pl.when(core == 1)
    def _():
        pair_copy(0).wait_send()

    @pl.when(core == 0)
    def _():
        pair_copy(1).wait_send()
        for step in range(1, X):
            rx_copy(step).wait_send()
        for step in range(1, Z):
            rz_copy(step).wait_send()

    @pl.loop(0, PIECES)
    def _(p):
        for k in range(Y):
            x_copy(k, p).wait_send()

    @pl.loop(0, HALF)
    def _(i):
        for stage in range(2):
            for way in range(2):
                y_copy(stage, way, i, ya.at[way, i]).wait_send()

    @pl.loop(0, HALF)
    def _(i):
        for way in range(2):
            p = (i, HALF + i)[way]
            y_copy(2, way, i, yc.at[way, i]).wait_recv()
            out_m[0, :, columns(p)] = base[p] + yc[way, i] * 0.125
        for way in range(2):
            y_copy(2, way, i, yc.at[way, i]).wait_send()


def write_out(new_m, new_u, out_m, out_u, sem):
    copy_m = pltpu.make_async_copy(new_m, out_m, sem.at[0])
    copy_u = pltpu.make_async_copy(new_u, out_u, sem.at[1])
    copy_m.start()
    copy_u.start()
    copy_m.wait()
    copy_u.wait()


def per_device(raw_grads, momentum, positions):
    piece = (BLOCK, COLS)
    tiles = (TILES, 8, 128)
    dma = pltpu.SemaphoreType.DMA
    shapes = ((1, BLOCK, WIDTH), (BLOCK, WIDTH))
    anywhere = pl.BlockSpec(memory_space=pl.ANY)
    inputs = (raw_grads, momentum, positions.T, jnp.asarray(dct_tables()))
    results = pl.pallas_call(
        kernel,
        out_shape=tuple(pltpu.VMEM(shape, F32) for shape in shapes),
        in_specs=[anywhere] * 4,
        out_specs=tuple(pl.BlockSpec(memory_space=pltpu.VMEM) for _ in shapes),
        scratch_shapes=[
            pltpu.VMEM((Y, 2, BLOCK, WIDTH), BF16),
            pltpu.VMEM((BLOCK, WIDTH), F32),
            pltpu.VMEM((KEEP, WIDTH // BLOCK), jnp.int32),
            pltpu.VMEM((BLOCK, 2 * BLOCK), BF16),
            pltpu.VMEM((Y, PIECES) + piece, F32),
            pltpu.VMEM((Y, PIECES) + piece, F32),
            pltpu.VMEM((2, HALF) + piece, F32),
            pltpu.VMEM((2, HALF) + piece, F32),
            pltpu.VMEM((2, HALF) + piece, F32),
            pltpu.VMEM((PIECES,) + piece, F32),
            pltpu.VMEM((3,) + tiles, F32),
            pltpu.VMEM((3, PIECES, ROWS, 256), BF16),
            pltpu.VMEM((3, PIECES, ROWS, 128), F32),
            pltpu.VMEM((PIECES, SPANS // 2, BLOCK, 256), BF16),
            pltpu.VMEM((2,) + tiles, F32),
            pltpu.VMEM((2,) + tiles, F32),
            pltpu.VMEM((X, CORES) + tiles, F32),
            pltpu.VMEM((Z, CORES) + tiles, F32),
            pltpu.VMEM((CORES,) + tiles, F32),
            dma((Y, 2)), dma((3,)), pltpu.SemaphoreType.REGULAR,
            dma((Y, PIECES)), dma((Y, PIECES)),
            dma((3, 2, HALF)), dma((3, 2, HALF)),
            dma((2,)), dma((2,)), dma((2,)), dma((2,)),
            dma((X - 1,)), dma((X - 1,)), dma((Z - 1,)), dma((Z - 1,)),
            dma((2,)), dma((2,)),
        ],
        compiler_params=pltpu.CompilerParams(
            collective_id=0, has_side_effects=True, vmem_limit_bytes=48 * 1024 * 1024),
    )(*(pltpu.with_memory_space_constraint(v, pltpu.HBM) for v in inputs))
    return pl.pallas_call(
        write_out,
        out_shape=tuple(pltpu.HBM(shape, F32) for shape in shapes),
        in_specs=[anywhere] * 2,
        out_specs=(anywhere, anywhere),
        scratch_shapes=[dma((2,))],
        compiler_params=pltpu.CompilerParams(vmem_limit_bytes=4 * 1024 * 1024),
    )(*(pltpu.with_memory_space_constraint(v, pltpu.VMEM) for v in results))


def solution(mesh):
    placed = (P(("rep", "fsdp"), None, None), P("rep", None, "fsdp"), P("fsdp", None))
    return jax.shard_map(
        per_device,
        mesh=mesh,
        in_specs=placed,
        out_specs=(P("rep", None, "fsdp"), P(None, "fsdp")),
        check_vma=False,
    )
```

```python
import math

import jax
import jax.numpy as jnp
import ml_dtypes
import numpy as np
from jax import lax
from jax.experimental import pallas as pl
from jax.experimental.pallas import tpu as pltpu
from jax.sharding import PartitionSpec as P

MESH = pl.DeviceIdType.MESH
F32, BF16 = jnp.float32, jnp.bfloat16

BLOCK = 64
KEEP = 32
X, Y, Z, CORES = 4, 4, 8, 2
WIDTH = 4096
PIECES = 8
HALF = PIECES // 2
COLS = WIDTH // PIECES
SPANS = COLS // BLOCK
ROWS = SPANS * KEEP
TILES = PIECES * SPANS * KEEP // (8 * 128)
AHEAD, BEHIND, ACROSS = 1, 3, 2
X_STEPS, Z_STEPS = (2, 1, 3), (4, 3, 5, 2, 6, 1, 7)
EARLY = 1


def dct_tables():
    k = np.arange(BLOCK)[:, None]
    j = np.arange(BLOCK)[None, :]
    cosines = np.cos(np.pi * (j + 0.5) * k / BLOCK) * math.sqrt(2.0 / BLOCK)
    cosines = np.where(k == 0, cosines * math.sqrt(0.5), cosines)
    high = cosines.astype(ml_dtypes.bfloat16)
    low = (cosines - high.astype(np.float64)).astype(ml_dtypes.bfloat16)
    return np.concatenate([high, low], axis=1)


def split(x):
    high = x.astype(BF16)
    return high, (x - high.astype(F32)).astype(BF16)


def lanes(shape):
    return lax.broadcasted_iota(jnp.int32, shape, 1)


def own_lane(piece):
    row = lax.broadcasted_iota(jnp.int32, (ROWS, 128), 0)
    return lanes((ROWS, 128)) == lax.rem(row, KEEP) + KEEP * lax.rem(piece, 4)


def unpack(tile, piece):
    wide = jnp.broadcast_to(tile[:, None, :], (SPANS, KEEP, 128)).reshape(ROWS, 128)
    return jnp.sum(jnp.where(own_lane(piece), wide, 0.0), axis=1, keepdims=True)


def pack(column, piece):
    wide = jnp.where(own_lane(piece), column, 0.0)
    return jnp.sum(wide.reshape(SPANS, KEEP, 128), axis=1)


def kernel(
    raw, mom, pos, cos, out_m, out_u,
    raw_v, mom_v, pos_v, cos_v, xsend, part, ya, yb, yc, base,
    places, left, right, left_t, csend, crecv, xslots, zslots, total,
    raw_sem, in_sem, go_sem, near_sem, x_send_sem, x_recv_sem, y_send_sem, y_recv_sem,
    p_send_sem, p_recv_sem, c_send_sem, c_recv_sem,
    rx_send_sem, rx_recv_sem, rz_send_sem, rz_recv_sem, pair_send_sem, pair_recv_sem,
):
    rep, fs = lax.axis_index("rep"), lax.axis_index("fsdp")
    y, core = fs // CORES, lax.rem(fs, CORES)
    x, z = rep // Z, lax.rem(rep, Z)

    def y_peer(step, of=core):
        return (rep, lax.rem(y + step, Y) * CORES + of)

    def x_peer(step):
        return (lax.rem(x + step, X) * Z + z, fs)

    def z_peer(step):
        return (x * Z + lax.rem(z + step, Z), fs)

    sibling = (rep, y * CORES + 1 - core)

    barrier = pltpu.get_barrier_semaphore()
    odd = lax.rem(y, 2) == 1

    def greet(peer):
        pl.semaphore_signal(barrier, inc=1, device_id=peer, device_id_type=MESH)

    @pl.when(jnp.logical_not(odd))
    def _():
        greet(y_peer(AHEAD, 1))
        greet(y_peer(BEHIND, 1))

    @pl.when(core == 0)
    def _():
        greet(sibling)

    def raw_copy(k, slot):
        owner = lax.rem(y + k, Y) * CORES + (core if slot == 0 else 1 - core)
        start = pl.multiple_of(owner * WIDTH, WIDTH)
        return pltpu.make_async_copy(
            raw.at[0, :, pl.ds(start, WIDTH)], raw_v.at[k, slot], raw_sem.at[k, slot])

    order = (ACROSS, BEHIND, AHEAD, 0)
    pos_copy = pltpu.make_async_copy(pos, pos_v, in_sem.at[0])
    cos_copy = pltpu.make_async_copy(cos, cos_v, in_sem.at[1])
    mom_copy = pltpu.make_async_copy(mom.at[0], mom_v, in_sem.at[2])
    raw_copy(ACROSS, 1).start()
    pos_copy.start()
    raw_copy(ACROSS, 0).start()

    def columns(piece):
        return pl.ds(pl.multiple_of(piece * COLS, COLS), COLS)

    def x_copy(k, p):
        return pltpu.make_async_remote_copy(
            xsend.at[k, p], part.at[k, p], x_send_sem.at[k, p], x_recv_sem.at[k, p],
            device_id=sibling, device_id_type=MESH)

    def widen(k, p):
        xsend[k, p] = raw_v[k, 1, :, columns(p)].astype(F32)

    pos_copy.wait()
    found = pos_v[...].astype(F32).T
    for m in range(TILES):
        places[0, m] = jnp.concatenate(
            [found[8 * (4 * m + j):8 * (4 * m + j) + 8] for j in range(4)], axis=1)

    def p_copy(way):
        return pltpu.make_async_remote_copy(
            places.at[0], places.at[1 + way], p_send_sem.at[way], p_recv_sem.at[way],
            device_id=y_peer((AHEAD, BEHIND)[way]), device_id_type=MESH)

    raw_copy(ACROSS, 1).wait()

    @pl.loop(0, PIECES)
    def _(p):
        widen(ACROSS, p)

    def tell(sem, peer):
        pl.semaphore_signal(sem, inc=1, device_id=peer, device_id_type=MESH)

    @pl.when(core == 1)
    def _():
        @pl.when(odd)
        def _():
            pl.semaphore_wait(barrier, 5)
            for step in (AHEAD, BEHIND):
                for of in range(CORES):
                    tell(near_sem, y_peer(step, of))

        @pl.when(jnp.logical_not(odd))
        def _():
            pl.semaphore_wait(barrier, 1)

        tell(go_sem, sibling)

    @pl.when(core == 0)
    def _():
        pl.semaphore_wait(go_sem, 1)

    @pl.loop(0, HALF)
    def _(i):
        x_copy(ACROSS, i).start()
        x_copy(ACROSS, HALF + i).start()

    for k in order[1:]:
        raw_copy(k, 1).start()
        raw_copy(k, 0).start()
    cos_copy.start()
    mom_copy.start()

    @pl.when(jnp.logical_not(odd))
    def _():
        pl.semaphore_wait(near_sem, 2)

    for way in range(2):
        p_copy(way).start()

    def y_copy(stage, way, i, src):
        dst = (ya, yb, yc)[stage]
        return pltpu.make_async_remote_copy(
            src, dst.at[way, i], y_send_sem.at[stage, way, i], y_recv_sem.at[stage, way, i],
            device_id=y_peer((BEHIND, AHEAD)[way]), device_id_type=MESH)

    def add_sibling(k, p):
        x_copy(k, p).wait_recv()
        part[k, p] = part[k, p] + raw_v[k, 0, :, columns(p)].astype(F32)

    def source(stage, way, i):
        if stage == 0:
            return ACROSS, (i, HALF + i)[way]
        if stage == 1:
            return (BEHIND, AHEAD)[way], (HALF + i, i)[way]
        return (BEHIND, AHEAD)[way], (i, HALF + i)[way]

    def prepare(who, p, transposed):
        place = unpack(places[who, p // 4], p).astype(jnp.int32)
        column = lanes((ROWS, BLOCK))
        pick_row = jnp.where(column == lax.shift_right_logical(place, 6), 1.0, 0.0)
        pick_col = jnp.where(column == lax.bitwise_and(place, 63), 1.0, 0.0)
        rows = jnp.dot(pick_row.astype(BF16), cos_v[...], preferred_element_type=F32)
        cols = jnp.dot(pick_col.astype(BF16), cos_v[...], preferred_element_type=F32)
        lane = lanes((ROWS, 128))
        turned = pltpu.roll(rows, 64, 1)
        left[who, p, :, 0:128] = jnp.where(lane < 64, rows, turned).astype(BF16)
        left[who, p, :, 128:256] = jnp.where(lane < 64, turned, rows).astype(BF16)
        odd = lax.rem(lax.broadcasted_iota(jnp.int32, (ROWS, 128), 0) // KEEP, 2)
        both = cols + pltpu.roll(cols, 64, 1)
        right[who, p] = jnp.where(lane // 64 == odd, both, 0.0)
        if transposed:
            for q in range(SPANS // 2):
                flat = rows[64 * q:64 * q + 64].T
                high, low = flat[0:64].astype(BF16), flat[64:128].astype(BF16)
                left_t[p, q] = jnp.concatenate([high, high, low, low], axis=1)

    def coefficients(field, who, p):
        found = []
        for h in range(2):
            high, low = split(field[:, 256 * h:256 * h + 256])
            spread = jnp.concatenate([high, low, high, low], axis=0)
            t = jnp.dot(left[who, p, 128 * h:128 * h + 128, :], spread, preferred_element_type=F32)
            t = jnp.concatenate([t[0:64, 0:128], t[64:128, 128:256]], axis=0)
            found.append(jnp.sum(t * right[who, p, 128 * h:128 * h + 128, :], axis=1, keepdims=True))
        return jnp.concatenate(found, axis=0)

    raw_copy(ACROSS, 0).wait()

    @pl.loop(0, HALF)
    def _(i):
        for way in range(2):
            k, p = source(0, way, i)
            add_sibling(k, p)
            y_copy(0, way, i, part.at[k, p]).start()

    for k in order[1:]:
        raw_copy(k, 1).wait()

        @pl.loop(0, HALF)
        def _(i):
            for p in (i, HALF + i):
                widen(k, p)
                x_copy(k, p).start()

    @pl.when(core == 0)
    def _():
        for step in range(1, X):
            greet(x_peer(step))
        for step in range(1, Z):
            greet(z_peer(step))

    for k in order[1:]:
        raw_copy(k, 0).wait()

    @pl.loop(0, EARLY)
    def _(i):
        for way in range(2):
            k, p = source(1, way, i)
            add_sibling(k, p)
            y_copy(1, way, i, part.at[k, p]).start()

    cos_copy.wait()
    for way in range(2):
        p_copy(way).wait_recv()

    for who in (1, 2):
        @pl.loop(0, PIECES, unroll=4)
        def _(p):
            prepare(who, p, False)

    @pl.loop(EARLY, HALF)
    def _(i):
        for way in range(2):
            add_sibling(*source(1, way, i))

    csend[...] = jnp.zeros((2, TILES, 8, 128), F32)

    def add_coefficients(way, k, p):
        csend[way, p // 4] += pack(coefficients(part[k, p], (1, 2)[way], p), p)

    @pl.loop(0, HALF)
    def _(i):
        for way in range(2):
            add_coefficients(way, *source(1, way, i))

    @pl.loop(0, HALF)
    def _(i):
        for way in range(2):
            add_sibling(*source(2, way, i))

    mom_copy.wait()

    @pl.loop(0, PIECES)
    def _(p):
        x_copy(0, p).wait_recv()
        summed = part[0, p] + raw_v[0, 0, :, columns(p)].astype(F32)
        base[p] = 0.999 * mom_v[:, columns(p)] + summed * 0.125

    @pl.loop(0, PIECES, unroll=2)
    def _(p):
        prepare(0, p, True)

    @pl.loop(0, HALF)
    def _(i):
        for way in range(2):
            k, p = source(2, way, i)
            y_copy(0, way, i, ya.at[way, i]).wait_recv()
            part[k, p] = part[k, p] + ya[way, i]
        for way in range(2):
            add_coefficients(way, *source(2, way, i))

    def c_copy(way):
        return pltpu.make_async_remote_copy(
            csend.at[way], crecv.at[way], c_send_sem.at[way], c_recv_sem.at[way],
            device_id=y_peer((BEHIND, AHEAD)[way]), device_id_type=MESH)

    for way in range(2):
        c_copy(way).start()

    def send_rest():
        @pl.loop(EARLY, HALF)
        def _(i):
            for way in range(2):
                k, p = source(1, way, i)
                y_copy(1, way, i, part.at[k, p]).start()

        @pl.loop(0, HALF)
        def _(i):
            for way in range(2):
                k, p = source(2, way, i)
                y_copy(2, way, i, part.at[k, p]).start()

    pl.when(core == 1)(send_rest)

    xslots[x, core] = jnp.zeros((TILES, 8, 128), F32)

    @pl.loop(0, PIECES, unroll=2)
    def _(p):
        xslots[x, core, p // 4] += pack(coefficients(base[p], 0, p), p)

    for way in range(2):
        c_copy(way).wait_recv()
    xslots[x, core] = xslots[x, core] + (crecv[0] + crecv[1]) * 0.125

    def pair_copy(back):
        ref = total.at[1] if back else xslots.at[x, 1]
        return pltpu.make_async_remote_copy(
            ref, ref, pair_send_sem.at[back], pair_recv_sem.at[back],
            device_id=sibling, device_id_type=MESH)

    def rx_copy(step):
        return pltpu.make_async_remote_copy(
            xslots.at[x], xslots.at[x], rx_send_sem.at[step - 1], rx_recv_sem.at[step - 1],
            device_id=x_peer(step), device_id_type=MESH)

    def rz_copy(step):
        return pltpu.make_async_remote_copy(
            zslots.at[z], zslots.at[z], rz_send_sem.at[step - 1], rz_recv_sem.at[step - 1],
            device_id=z_peer(step), device_id_type=MESH)

    @pl.when(core == 1)
    def _():
        pair_copy(0).start()

    @pl.when(core == 0)
    def _():
        pl.semaphore_wait(barrier, X - 1 + Z - 1)
        pair_copy(0).wait_recv()
        for step in X_STEPS:
            rx_copy(step).start()

    def inverse(p, q, column):
        high, low = split(column * right[0, p, 64 * q:64 * q + 64, :])
        spread = jnp.concatenate([high, low, high, low], axis=0)
        return jnp.dot(left_t[p, q], spread, preferred_element_type=F32)

    @pl.loop(0, PIECES, unroll=4)
    def _(p):
        column = unpack(xslots[x, core, p // 4], p)
        for q in range(SPANS // 2):
            base[p, :, 128 * q:128 * q + 128] -= inverse(p, q, column[64 * q:64 * q + 64])

    @pl.when(core == 0)
    def _():
        for step in range(1, X):
            rx_copy(step).wait_recv()
        send_rest()
        zslots[z] = (xslots[0] + xslots[1]) + (xslots[2] + xslots[3])
        for step in Z_STEPS:
            rz_copy(step).start()
        for step in range(1, Z):
            rz_copy(step).wait_recv()
        summed = zslots[0]
        for s in range(1, Z):
            summed = summed + zslots[s]
        total[...] = summed
        pair_copy(1).start()

    @pl.when(core == 1)
    def _():
        pair_copy(1).wait_recv()

    @pl.loop(0, PIECES, unroll=4)
    def _(p):
        column = unpack(total[core, p // 4], p)
        mean = jnp.sum((column * column).reshape(SPANS, KEEP, 1), axis=1, keepdims=True)
        scale = 1.0 / jnp.sqrt(mean * (1.0 / (BLOCK * BLOCK)) + 1e-06)
        column = column * jnp.broadcast_to(scale, (SPANS, KEEP, 1)).reshape(ROWS, 1)
        for q in range(SPANS // 2):
            at = pl.ds(pl.multiple_of(p * COLS + 128 * q, 128), 128)
            out_u[:, at] = jnp.tanh(inverse(p, q, column[64 * q:64 * q + 64]))

    @pl.loop(0, HALF)
    def _(i):
        for way in range(2):
            p = (HALF + i, i)[way]
            y_copy(1, way, i, yb.at[way, i]).wait_recv()
            base[p] += yb[way, i] * 0.125

    for way in range(2):
        p_copy(way).wait_send()
        c_copy(way).wait_send()

    @pl.when(core == 1)
    def _():
        pair_copy(0).wait_send()

    @pl.when(core == 0)
    def _():
        pair_copy(1).wait_send()
        for step in range(1, X):
            rx_copy(step).wait_send()
        for step in range(1, Z):
            rz_copy(step).wait_send()

    @pl.loop(0, PIECES)
    def _(p):
        for k in range(Y):
            x_copy(k, p).wait_send()

    @pl.loop(0, HALF)
    def _(i):
        for stage in range(2):
            for way in range(2):
                y_copy(stage, way, i, ya.at[way, i]).wait_send()

    @pl.loop(0, HALF)
    def _(i):
        for way in range(2):
            p = (i, HALF + i)[way]
            y_copy(2, way, i, yc.at[way, i]).wait_recv()
            out_m[0, :, columns(p)] = base[p] + yc[way, i] * 0.125
        for way in range(2):
            y_copy(2, way, i, yc.at[way, i]).wait_send()


def write_out(new_m, new_u, out_m, out_u, sem):
    copy_m = pltpu.make_async_copy(new_m, out_m, sem.at[0])
    copy_u = pltpu.make_async_copy(new_u, out_u, sem.at[1])
    copy_m.start()
    copy_u.start()
    copy_m.wait()
    copy_u.wait()


def per_device(raw_grads, momentum, positions):
    piece = (BLOCK, COLS)
    tiles = (TILES, 8, 128)
    dma = pltpu.SemaphoreType.DMA
    shapes = ((1, BLOCK, WIDTH), (BLOCK, WIDTH))
    anywhere = pl.BlockSpec(memory_space=pl.ANY)
    inputs = (raw_grads, momentum, positions.T, jnp.asarray(dct_tables()))
    results = pl.pallas_call(
        kernel,
        out_shape=tuple(pltpu.VMEM(shape, F32) for shape in shapes),
        in_specs=[anywhere] * 4,
        out_specs=tuple(pl.BlockSpec(memory_space=pltpu.VMEM) for _ in shapes),
        scratch_shapes=[
            pltpu.VMEM((Y, 2, BLOCK, WIDTH), BF16),
            pltpu.VMEM((BLOCK, WIDTH), F32),
            pltpu.VMEM((KEEP, WIDTH // BLOCK), jnp.int32),
            pltpu.VMEM((BLOCK, 2 * BLOCK), BF16),
            pltpu.VMEM((Y, PIECES) + piece, F32),
            pltpu.VMEM((Y, PIECES) + piece, F32),
            pltpu.VMEM((2, HALF) + piece, F32),
            pltpu.VMEM((2, HALF) + piece, F32),
            pltpu.VMEM((2, HALF) + piece, F32),
            pltpu.VMEM((PIECES,) + piece, F32),
            pltpu.VMEM((3,) + tiles, F32),
            pltpu.VMEM((3, PIECES, ROWS, 256), BF16),
            pltpu.VMEM((3, PIECES, ROWS, 128), F32),
            pltpu.VMEM((PIECES, SPANS // 2, BLOCK, 256), BF16),
            pltpu.VMEM((2,) + tiles, F32),
            pltpu.VMEM((2,) + tiles, F32),
            pltpu.VMEM((X, CORES) + tiles, F32),
            pltpu.VMEM((Z, CORES) + tiles, F32),
            pltpu.VMEM((CORES,) + tiles, F32),
            dma((Y, 2)), dma((3,)), pltpu.SemaphoreType.REGULAR, pltpu.SemaphoreType.REGULAR,
            dma((Y, PIECES)), dma((Y, PIECES)),
            dma((3, 2, HALF)), dma((3, 2, HALF)),
            dma((2,)), dma((2,)), dma((2,)), dma((2,)),
            dma((X - 1,)), dma((X - 1,)), dma((Z - 1,)), dma((Z - 1,)),
            dma((2,)), dma((2,)),
        ],
        compiler_params=pltpu.CompilerParams(
            collective_id=0, has_side_effects=True, vmem_limit_bytes=48 * 1024 * 1024),
    )(*(pltpu.with_memory_space_constraint(v, pltpu.HBM) for v in inputs))
    return pl.pallas_call(
        write_out,
        out_shape=tuple(pltpu.HBM(shape, F32) for shape in shapes),
        in_specs=[anywhere] * 2,
        out_specs=(anywhere, anywhere),
        scratch_shapes=[dma((2,))],
        compiler_params=pltpu.CompilerParams(vmem_limit_bytes=4 * 1024 * 1024),
    )(*(pltpu.with_memory_space_constraint(v, pltpu.VMEM) for v in results))


def solution(mesh):
    placed = (P(("rep", "fsdp"), None, None), P("rep", None, "fsdp"), P("fsdp", None))
    return jax.shard_map(
        per_device,
        mesh=mesh,
        in_specs=placed,
        out_specs=(P("rep", None, "fsdp"), P(None, "fsdp")),
        check_vma=False,
    )
```

```python
import math

import jax
import jax.numpy as jnp
import ml_dtypes
import numpy as np
from jax import lax
from jax.experimental import pallas as pl
from jax.experimental.pallas import tpu as pltpu
from jax.sharding import PartitionSpec as P

MESH = pl.DeviceIdType.MESH
F32, BF16 = jnp.float32, jnp.bfloat16

BLOCK = 64
KEEP = 32
X, Y, Z, CORES = 4, 4, 8, 2
WIDTH = 4096
PIECES = 8
HALF = PIECES // 2
LAST = HALF - 1
COLS = WIDTH // PIECES
SPANS = COLS // BLOCK
ROWS = SPANS * KEEP
TILES = PIECES * SPANS * KEEP // (8 * 128)
AHEAD, BEHIND, ACROSS = 1, 3, 2
X_STEPS, Z_STEPS = (2, 1, 3), (4, 3, 5, 2, 6, 1, 7)
EARLY = 1


def dct_tables():
    k = np.arange(BLOCK)[:, None]
    j = np.arange(BLOCK)[None, :]
    cosines = np.cos(np.pi * (j + 0.5) * k / BLOCK) * math.sqrt(2.0 / BLOCK)
    cosines = np.where(k == 0, cosines * math.sqrt(0.5), cosines)
    high = cosines.astype(ml_dtypes.bfloat16)
    low = (cosines - high.astype(np.float64)).astype(ml_dtypes.bfloat16)
    return np.concatenate([high, low], axis=1)


def split(x):
    high = x.astype(BF16)
    return high, (x - high.astype(F32)).astype(BF16)


def lanes(shape):
    return lax.broadcasted_iota(jnp.int32, shape, 1)


def own_lane(piece):
    row = lax.broadcasted_iota(jnp.int32, (ROWS, 128), 0)
    return lanes((ROWS, 128)) == lax.rem(row, KEEP) + KEEP * lax.rem(piece, 4)


def unpack(tile, piece):
    wide = jnp.broadcast_to(tile[:, None, :], (SPANS, KEEP, 128)).reshape(ROWS, 128)
    return jnp.sum(jnp.where(own_lane(piece), wide, 0.0), axis=1, keepdims=True)


def pack(column, piece):
    wide = jnp.where(own_lane(piece), column, 0.0)
    return jnp.sum(wide.reshape(SPANS, KEEP, 128), axis=1)


def kernel(
    raw, mom, pos, cos, out_m, out_u,
    raw_v, mom_v, pos_v, cos_v, xsend, part, ya, yh, yb, yc, base,
    places, left, right, left_t, csend, crecv, xslots, zslots, total,
    raw_sem, in_sem, go_sem, near_sem, x_send_sem, x_recv_sem, y_send_sem, y_recv_sem, h_send_sem, h_recv_sem,
    p_send_sem, p_recv_sem, c_send_sem, c_recv_sem,
    rx_send_sem, rx_recv_sem, rz_send_sem, rz_recv_sem, pair_send_sem, pair_recv_sem,
):
    rep, fs = lax.axis_index("rep"), lax.axis_index("fsdp")
    y, core = fs // CORES, lax.rem(fs, CORES)
    x, z = rep // Z, lax.rem(rep, Z)

    def y_peer(step, of=core):
        return (rep, lax.rem(y + step, Y) * CORES + of)

    def x_peer(step):
        return (lax.rem(x + step, X) * Z + z, fs)

    def z_peer(step):
        return (x * Z + lax.rem(z + step, Z), fs)

    sibling = (rep, y * CORES + 1 - core)

    barrier = pltpu.get_barrier_semaphore()
    odd = lax.rem(y, 2) == 1

    def greet(peer):
        pl.semaphore_signal(barrier, inc=1, device_id=peer, device_id_type=MESH)

    @pl.when(jnp.logical_not(odd))
    def _():
        greet(y_peer(AHEAD, 1))
        greet(y_peer(BEHIND, 1))

    @pl.when(core == 0)
    def _():
        greet(sibling)

    def raw_copy(k, slot):
        owner = lax.rem(y + k, Y) * CORES + (core if slot == 0 else 1 - core)
        start = pl.multiple_of(owner * WIDTH, WIDTH)
        return pltpu.make_async_copy(
            raw.at[0, :, pl.ds(start, WIDTH)], raw_v.at[k, slot], raw_sem.at[k, slot])

    order = (ACROSS, BEHIND, AHEAD, 0)
    pos_copy = pltpu.make_async_copy(pos, pos_v, in_sem.at[0])
    cos_copy = pltpu.make_async_copy(cos, cos_v, in_sem.at[1])
    mom_copy = pltpu.make_async_copy(mom.at[0], mom_v, in_sem.at[2])
    raw_copy(ACROSS, 1).start()
    pos_copy.start()
    raw_copy(ACROSS, 0).start()

    def columns(piece):
        return pl.ds(pl.multiple_of(piece * COLS, COLS), COLS)

    def x_copy(k, p):
        return pltpu.make_async_remote_copy(
            xsend.at[k, p], part.at[k, p], x_send_sem.at[k, p], x_recv_sem.at[k, p],
            device_id=sibling, device_id_type=MESH)

    def widen(k, p):
        xsend[k, p] = raw_v[k, 1, :, columns(p)].astype(F32)

    def tell(sem, peer):
        pl.semaphore_signal(sem, inc=1, device_id=peer, device_id_type=MESH)

    @pl.when(core == 1)
    def _():
        @pl.when(odd)
        def _():
            pl.semaphore_wait(barrier, 5)
            for step in (AHEAD, BEHIND):
                for of in range(CORES):
                    tell(near_sem, y_peer(step, of))

        @pl.when(jnp.logical_not(odd))
        def _():
            pl.semaphore_wait(barrier, 1)

        tell(go_sem, sibling)

    @pl.when(core == 0)
    def _():
        pl.semaphore_wait(go_sem, 1)

    raw_copy(ACROSS, 1).wait()

    @pl.loop(0, HALF)
    def _(i):
        for p in (i, PIECES - 1 - i):
            widen(ACROSS, p)
            x_copy(ACROSS, p).start()

    for k in order[1:]:
        raw_copy(k, 1).start()
        raw_copy(k, 0).start()
    cos_copy.start()
    mom_copy.start()

    pos_copy.wait()
    found = pos_v[...].astype(F32).T
    for m in range(TILES):
        places[0, m] = jnp.concatenate(
            [found[8 * (4 * m + j):8 * (4 * m + j) + 8] for j in range(4)], axis=1)

    def p_copy(way):
        return pltpu.make_async_remote_copy(
            places.at[0], places.at[1 + way], p_send_sem.at[way], p_recv_sem.at[way],
            device_id=y_peer((AHEAD, BEHIND)[way]), device_id_type=MESH)

    @pl.when(jnp.logical_not(odd))
    def _():
        pl.semaphore_wait(near_sem, 2)

    for way in range(2):
        p_copy(way).start()

    def y_copy(stage, way, i, src):
        dst = (ya, yb, yc)[stage]
        return pltpu.make_async_remote_copy(
            src, dst.at[way, i], y_send_sem.at[stage, way, i], y_recv_sem.at[stage, way, i],
            device_id=y_peer((BEHIND, AHEAD)[way]), device_id_type=MESH)

    def add_sibling(k, p):
        x_copy(k, p).wait_recv()
        part[k, p] = part[k, p] + raw_v[k, 0, :, columns(p)].astype(F32)

    def source(stage, way, i):
        low, high = i, PIECES - 1 - i
        if stage == 0:
            return ACROSS, (low, high)[way]
        if stage == 1:
            return (BEHIND, AHEAD)[way], (high, low)[way]
        return (BEHIND, AHEAD)[way], (low, high)[way]

    def prepare(who, p, transposed):
        place = unpack(places[who, p // 4], p).astype(jnp.int32)
        column = lanes((ROWS, BLOCK))
        pick_row = jnp.where(column == lax.shift_right_logical(place, 6), 1.0, 0.0)
        pick_col = jnp.where(column == lax.bitwise_and(place, 63), 1.0, 0.0)
        rows = jnp.dot(pick_row.astype(BF16), cos_v[...], preferred_element_type=F32)
        cols = jnp.dot(pick_col.astype(BF16), cos_v[...], preferred_element_type=F32)
        lane = lanes((ROWS, 128))
        turned = pltpu.roll(rows, 64, 1)
        left[who, p, :, 0:128] = jnp.where(lane < 64, rows, turned).astype(BF16)
        left[who, p, :, 128:256] = jnp.where(lane < 64, turned, rows).astype(BF16)
        odd = lax.rem(lax.broadcasted_iota(jnp.int32, (ROWS, 128), 0) // KEEP, 2)
        both = cols + pltpu.roll(cols, 64, 1)
        right[who, p] = jnp.where(lane // 64 == odd, both, 0.0)
        if transposed:
            for q in range(SPANS // 2):
                flat = rows[64 * q:64 * q + 64].T
                high, low = flat[0:64].astype(BF16), flat[64:128].astype(BF16)
                left_t[p, q] = jnp.concatenate([high, high, low, low], axis=1)

    def coefficients(field, who, p):
        found = []
        for h in range(2):
            high, low = split(field[:, 256 * h:256 * h + 256])
            spread = jnp.concatenate([high, low, high, low], axis=0)
            t = jnp.dot(left[who, p, 128 * h:128 * h + 128, :], spread, preferred_element_type=F32)
            t = jnp.concatenate([t[0:64, 0:128], t[64:128, 128:256]], axis=0)
            found.append(jnp.sum(t * right[who, p, 128 * h:128 * h + 128, :], axis=1, keepdims=True))
        return jnp.concatenate(found, axis=0)

    raw_copy(ACROSS, 0).wait()

    shared = jnp.where(y == 1, LAST, HALF)
    halves = (pl.ds(0, COLS // 2), pl.ds(COLS // 2, COLS // 2))
    halving = jnp.logical_and(core == 0, lax.rem(y, 2) == 1)
    halved = jnp.logical_and(core == 0, lax.rem(y, 2) == 0)

    def h_copy(way):
        return pltpu.make_async_remote_copy(
            part.at[ACROSS, shared, :, halves[way]], yh.at[way], h_send_sem.at[way], h_recv_sem.at[way],
            device_id=y_peer((BEHIND, AHEAD)[way]), device_id_type=MESH)

    def whole(way):
        return jnp.logical_not(jnp.logical_and(core == 0, y == (1, 3)[way]))

    @pl.loop(0, LAST)
    def _(i):
        for way in range(2):
            k, p = source(0, way, i)
            add_sibling(k, p)
            y_copy(0, way, i, part.at[k, p]).start()

    for way in range(2):
        add_sibling(*source(0, way, LAST))

    for way in range(2):
        @pl.when(whole(way))
        def _():
            y_copy(0, way, LAST, part.at[source(0, way, LAST)]).start()

    @pl.when(halving)
    def _():
        for way in range(2):
            h_copy(way).start()

    for k in order[1:]:
        raw_copy(k, 1).wait()

        @pl.loop(0, HALF)
        def _(i):
            for p in (i, PIECES - 1 - i):
                widen(k, p)
                x_copy(k, p).start()

    @pl.when(core == 0)
    def _():
        for step in range(1, X):
            greet(x_peer(step))
        for step in range(1, Z):
            greet(z_peer(step))

    for k in order[1:]:
        raw_copy(k, 0).wait()

    @pl.loop(0, EARLY)
    def _(i):
        for way in range(2):
            k, p = source(1, way, i)
            add_sibling(k, p)
            y_copy(1, way, i, part.at[k, p]).start()

    cos_copy.wait()
    for way in range(2):
        p_copy(way).wait_recv()

    for who in (1, 2):
        @pl.loop(0, PIECES, unroll=4)
        def _(p):
            prepare(who, p, False)

    @pl.loop(EARLY, HALF)
    def _(i):
        for way in range(2):
            add_sibling(*source(1, way, i))

    csend[...] = jnp.zeros((2, TILES, 8, 128), F32)

    def add_coefficients(way, k, p):
        csend[way, p // 4] += pack(coefficients(part[k, p], (1, 2)[way], p), p)

    joined = jnp.logical_and(core == 0, y == 2)

    @pl.loop(0, LAST + jnp.where(joined, 0, 1))
    def _(i):
        for way in range(2):
            add_coefficients(way, *source(1, way, i))

    @pl.loop(0, HALF)
    def _(i):
        for way in range(2):
            add_sibling(*source(2, way, i))

    mom_copy.wait()

    @pl.loop(0, PIECES)
    def _(p):
        x_copy(0, p).wait_recv()
        summed = part[0, p] + raw_v[0, 0, :, columns(p)].astype(F32)
        base[p] = 0.999 * mom_v[:, columns(p)] + summed * 0.125

    @pl.loop(0, PIECES, unroll=2)
    def _(p):
        prepare(0, p, True)

    def relay(way, i):
        k, p = source(2, way, i)
        y_copy(0, way, i, ya.at[way, i]).wait_recv()
        part[k, p] = part[k, p] + ya[way, i]

    @pl.loop(0, LAST)
    def _(i):
        for way in range(2):
            relay(way, i)
        for way in range(2):
            add_coefficients(way, *source(2, way, i))

    @pl.when(jnp.logical_not(jnp.logical_and(core == 0, y == 0)))
    def _():
        for way in range(2):
            relay(way, LAST)

    @pl.when(halved)
    def _():
        for way in range(2):
            k, p = (BEHIND, AHEAD)[way], jnp.where(y == (0, 2)[way], LAST, HALF)
            h_copy(way).wait_recv()
            part[k, p, :, halves[way]] = part[k, p, :, halves[way]] + yh[way]

    for way in range(2):
        add_coefficients(way, *source(2, way, LAST))

    @pl.when(joined)
    def _():
        for way in range(2):
            add_coefficients(way, *source(1, way, LAST))

    def c_copy(way):
        return pltpu.make_async_remote_copy(
            csend.at[way], crecv.at[way], c_send_sem.at[way], c_recv_sem.at[way],
            device_id=y_peer((BEHIND, AHEAD)[way]), device_id_type=MESH)

    for way in range(2):
        c_copy(way).start()

    def send_rest():
        @pl.loop(EARLY, HALF)
        def _(i):
            for way in range(2):
                k, p = source(1, way, i)
                y_copy(1, way, i, part.at[k, p]).start()

        @pl.loop(0, HALF)
        def _(i):
            for way in range(2):
                k, p = source(2, way, i)
                y_copy(2, way, i, part.at[k, p]).start()

    pl.when(core == 1)(send_rest)

    xslots[x, core] = jnp.zeros((TILES, 8, 128), F32)

    @pl.loop(0, PIECES, unroll=2)
    def _(p):
        xslots[x, core, p // 4] += pack(coefficients(base[p], 0, p), p)

    for way in range(2):
        c_copy(way).wait_recv()
    xslots[x, core] = xslots[x, core] + (crecv[0] + crecv[1]) * 0.125

    def pair_copy(back):
        ref = total.at[1] if back else xslots.at[x, 1]
        return pltpu.make_async_remote_copy(
            ref, ref, pair_send_sem.at[back], pair_recv_sem.at[back],
            device_id=sibling, device_id_type=MESH)

    def rx_copy(step):
        return pltpu.make_async_remote_copy(
            xslots.at[x], xslots.at[x], rx_send_sem.at[step - 1], rx_recv_sem.at[step - 1],
            device_id=x_peer(step), device_id_type=MESH)

    def rz_copy(step):
        return pltpu.make_async_remote_copy(
            zslots.at[z], zslots.at[z], rz_send_sem.at[step - 1], rz_recv_sem.at[step - 1],
            device_id=z_peer(step), device_id_type=MESH)

    @pl.when(core == 1)
    def _():
        pair_copy(0).start()

    @pl.when(core == 0)
    def _():
        pl.semaphore_wait(barrier, X - 1 + Z - 1)
        pair_copy(0).wait_recv()
        for step in X_STEPS:
            rx_copy(step).start()

    def inverse(p, q, column):
        high, low = split(column * right[0, p, 64 * q:64 * q + 64, :])
        spread = jnp.concatenate([high, low, high, low], axis=0)
        return jnp.dot(left_t[p, q], spread, preferred_element_type=F32)

    @pl.loop(0, PIECES, unroll=4)
    def _(p):
        column = unpack(xslots[x, core, p // 4], p)
        for q in range(SPANS // 2):
            base[p, :, 128 * q:128 * q + 128] -= inverse(p, q, column[64 * q:64 * q + 64])

    @pl.when(core == 0)
    def _():
        for step in range(1, X):
            rx_copy(step).wait_recv()
        send_rest()
        zslots[z] = (xslots[0] + xslots[1]) + (xslots[2] + xslots[3])
        for step in Z_STEPS:
            rz_copy(step).start()
        for step in range(1, Z):
            rz_copy(step).wait_recv()
        summed = zslots[0]
        for s in range(1, Z):
            summed = summed + zslots[s]
        total[...] = summed
        pair_copy(1).start()

    @pl.when(core == 1)
    def _():
        pair_copy(1).wait_recv()

    @pl.loop(0, PIECES, unroll=4)
    def _(p):
        column = unpack(total[core, p // 4], p)
        mean = jnp.sum((column * column).reshape(SPANS, KEEP, 1), axis=1, keepdims=True)
        scale = 1.0 / jnp.sqrt(mean * (1.0 / (BLOCK * BLOCK)) + 1e-06)
        column = column * jnp.broadcast_to(scale, (SPANS, KEEP, 1)).reshape(ROWS, 1)
        for q in range(SPANS // 2):
            at = pl.ds(pl.multiple_of(p * COLS + 128 * q, 128), 128)
            out_u[:, at] = jnp.tanh(inverse(p, q, column[64 * q:64 * q + 64]))

    @pl.loop(0, HALF)
    def _(i):
        for way in range(2):
            p = (PIECES - 1 - i, i)[way]
            y_copy(1, way, i, yb.at[way, i]).wait_recv()
            base[p] += yb[way, i] * 0.125

    for way in range(2):
        p_copy(way).wait_send()
        c_copy(way).wait_send()

    @pl.when(core == 1)
    def _():
        pair_copy(0).wait_send()

    @pl.when(core == 0)
    def _():
        pair_copy(1).wait_send()
        for step in range(1, X):
            rx_copy(step).wait_send()
        for step in range(1, Z):
            rz_copy(step).wait_send()

    @pl.loop(0, PIECES)
    def _(p):
        for k in range(Y):
            x_copy(k, p).wait_send()

    @pl.loop(0, LAST)
    def _(i):
        for way in range(2):
            y_copy(0, way, i, ya.at[way, i]).wait_send()

    for way in range(2):
        @pl.when(whole(way))
        def _():
            y_copy(0, way, LAST, ya.at[way, LAST]).wait_send()

    @pl.when(halving)
    def _():
        for way in range(2):
            h_copy(way).wait_send()

    @pl.loop(0, HALF)
    def _(i):
        for way in range(2):
            y_copy(1, way, i, yb.at[way, i]).wait_send()

    @pl.loop(0, HALF)
    def _(i):
        for way in range(2):
            p = (i, PIECES - 1 - i)[way]
            y_copy(2, way, i, yc.at[way, i]).wait_recv()
            out_m[0, :, columns(p)] = base[p] + yc[way, i] * 0.125
        for way in range(2):
            y_copy(2, way, i, yc.at[way, i]).wait_send()


def write_out(new_m, new_u, out_m, out_u, sem):
    copy_m = pltpu.make_async_copy(new_m, out_m, sem.at[0])
    copy_u = pltpu.make_async_copy(new_u, out_u, sem.at[1])
    copy_m.start()
    copy_u.start()
    copy_m.wait()
    copy_u.wait()


def per_device(raw_grads, momentum, positions):
    piece = (BLOCK, COLS)
    tiles = (TILES, 8, 128)
    dma = pltpu.SemaphoreType.DMA
    shapes = ((1, BLOCK, WIDTH), (BLOCK, WIDTH))
    anywhere = pl.BlockSpec(memory_space=pl.ANY)
    inputs = (raw_grads, momentum, positions.T, jnp.asarray(dct_tables()))
    results = pl.pallas_call(
        kernel,
        out_shape=tuple(pltpu.VMEM(shape, F32) for shape in shapes),
        in_specs=[anywhere] * 4,
        out_specs=tuple(pl.BlockSpec(memory_space=pltpu.VMEM) for _ in shapes),
        scratch_shapes=[
            pltpu.VMEM((Y, 2, BLOCK, WIDTH), BF16),
            pltpu.VMEM((BLOCK, WIDTH), F32),
            pltpu.VMEM((KEEP, WIDTH // BLOCK), jnp.int32),
            pltpu.VMEM((BLOCK, 2 * BLOCK), BF16),
            pltpu.VMEM((Y, PIECES) + piece, F32),
            pltpu.VMEM((Y, PIECES) + piece, F32),
            pltpu.VMEM((2, HALF) + piece, F32),
            pltpu.VMEM((2, BLOCK, COLS // 2), F32),
            pltpu.VMEM((2, HALF) + piece, F32),
            pltpu.VMEM((2, HALF) + piece, F32),
            pltpu.VMEM((PIECES,) + piece, F32),
            pltpu.VMEM((3,) + tiles, F32),
            pltpu.VMEM((3, PIECES, ROWS, 256), BF16),
            pltpu.VMEM((3, PIECES, ROWS, 128), F32),
            pltpu.VMEM((PIECES, SPANS // 2, BLOCK, 256), BF16),
            pltpu.VMEM((2,) + tiles, F32),
            pltpu.VMEM((2,) + tiles, F32),
            pltpu.VMEM((X, CORES) + tiles, F32),
            pltpu.VMEM((Z, CORES) + tiles, F32),
            pltpu.VMEM((CORES,) + tiles, F32),
            dma((Y, 2)), dma((3,)), pltpu.SemaphoreType.REGULAR, pltpu.SemaphoreType.REGULAR,
            dma((Y, PIECES)), dma((Y, PIECES)),
            dma((3, 2, HALF)), dma((3, 2, HALF)), dma((2,)), dma((2,)),
            dma((2,)), dma((2,)), dma((2,)), dma((2,)),
            dma((X - 1,)), dma((X - 1,)), dma((Z - 1,)), dma((Z - 1,)),
            dma((2,)), dma((2,)),
        ],
        compiler_params=pltpu.CompilerParams(
            collective_id=0, has_side_effects=True, vmem_limit_bytes=48 * 1024 * 1024),
    )(*(pltpu.with_memory_space_constraint(v, pltpu.HBM) for v in inputs))
    return pl.pallas_call(
        write_out,
        out_shape=tuple(pltpu.HBM(shape, F32) for shape in shapes),
        in_specs=[anywhere] * 2,
        out_specs=(anywhere, anywhere),
        scratch_shapes=[dma((2,))],
        compiler_params=pltpu.CompilerParams(vmem_limit_bytes=4 * 1024 * 1024),
    )(*(pltpu.with_memory_space_constraint(v, pltpu.VMEM) for v in results))


def solution(mesh):
    placed = (P(("rep", "fsdp"), None, None), P("rep", None, "fsdp"), P("fsdp", None))
    return jax.shard_map(
        per_device,
        mesh=mesh,
        in_specs=placed,
        out_specs=(P("rep", None, "fsdp"), P(None, "fsdp")),
        check_vma=False,
    )
```

```python
import math

import jax
import jax.numpy as jnp
from jax import lax
from jax.experimental import pallas as pl
from jax.experimental.pallas import tpu as pltpu
from jax.sharding import PartitionSpec as P

MESH = pl.DeviceIdType.MESH
F32, BF16 = jnp.float32, jnp.bfloat16

BLOCK = 64
KEEP = 32
X, Y, Z, CORES = 4, 4, 8, 2
WIDTH = 4096
PIECES = 8
HALF = PIECES // 2
LAST = HALF - 1
COLS = WIDTH // PIECES
SPANS = COLS // BLOCK
ROWS = SPANS * KEEP
TILES = PIECES * SPANS * KEEP // (8 * 128)
AHEAD, BEHIND, ACROSS = 1, 3, 2
X_STEPS, Z_STEPS = (2, 1, 3), (4, 3, 5, 2, 6, 1, 7)
EARLY = 1


def split(x):
    high = x.astype(BF16)
    return high, (x - high.astype(F32)).astype(BF16)


def dct_table():
    k = lax.broadcasted_iota(jnp.int32, (BLOCK, BLOCK), 0)
    j = lax.broadcasted_iota(jnp.int32, (BLOCK, BLOCK), 1)
    turn = lax.rem((2 * j + 1) * k, 4 * BLOCK)
    cosines = jnp.cos(turn.astype(F32) * (math.pi / (2 * BLOCK))) * math.sqrt(2.0 / BLOCK)
    high, low = split(jnp.where(k == 0, cosines * math.sqrt(0.5), cosines))
    return jnp.concatenate([high, low], axis=1)


def lanes(shape):
    return lax.broadcasted_iota(jnp.int32, shape, 1)


def own_lane(piece):
    row = lax.broadcasted_iota(jnp.int32, (ROWS, 128), 0)
    return lanes((ROWS, 128)) == lax.rem(row, KEEP) + KEEP * lax.rem(piece, 4)


def unpack(tile, piece):
    wide = jnp.broadcast_to(tile[:, None, :], (SPANS, KEEP, 128)).reshape(ROWS, 128)
    return jnp.sum(jnp.where(own_lane(piece), wide, 0.0), axis=1, keepdims=True)


def pack(column, piece):
    wide = jnp.where(own_lane(piece), column, 0.0)
    return jnp.sum(wide.reshape(SPANS, KEEP, 128), axis=1)


def kernel(
    raw, mom, pos, out_m, out_u,
    raw_v, mom_v, pos_v, cos_v, xsend, part, ya, yh, yb, yc, base,
    places, left, right, left_t, csend, crecv, xslots, zslots, total,
    raw_sem, in_sem, go_sem, near_sem, x_send_sem, x_recv_sem, y_send_sem, y_recv_sem, w_send_sem, w_recv_sem, h_send_sem, h_recv_sem,
    p_send_sem, p_recv_sem, c_send_sem, c_recv_sem,
    rx_send_sem, rx_recv_sem, rz_send_sem, rz_recv_sem, pair_send_sem, pair_recv_sem,
):
    rep, fs = lax.axis_index("rep"), lax.axis_index("fsdp")
    y, core = fs // CORES, lax.rem(fs, CORES)
    x, z = rep // Z, lax.rem(rep, Z)

    def y_peer(step, of=core):
        return (rep, lax.rem(y + step, Y) * CORES + of)

    def x_peer(step):
        return (lax.rem(x + step, X) * Z + z, fs)

    def z_peer(step):
        return (x * Z + lax.rem(z + step, Z), fs)

    sibling = (rep, y * CORES + 1 - core)

    barrier = pltpu.get_barrier_semaphore()
    odd = lax.rem(y, 2) == 1

    def greet(peer):
        pl.semaphore_signal(barrier, inc=1, device_id=peer, device_id_type=MESH)

    @pl.when(jnp.logical_not(odd))
    def _():
        greet(y_peer(AHEAD, 1))
        greet(y_peer(BEHIND, 1))

    @pl.when(core == 0)
    def _():
        greet(sibling)

    def raw_copy(k, slot):
        owner = lax.rem(y + k, Y) * CORES + (core if slot == 0 else 1 - core)
        start = pl.multiple_of(owner * WIDTH, WIDTH)
        return pltpu.make_async_copy(
            raw.at[0, :, pl.ds(start, WIDTH)], raw_v.at[k, slot], raw_sem.at[k, slot])

    order = (ACROSS, BEHIND, AHEAD, 0)
    pos_copy = pltpu.make_async_copy(pos, pos_v, in_sem.at[0])
    mom_copy = pltpu.make_async_copy(mom.at[0], mom_v, in_sem.at[1])
    raw_copy(ACROSS, 1).start()
    pos_copy.start()
    raw_copy(ACROSS, 0).start()

    def columns(piece):
        return pl.ds(pl.multiple_of(piece * COLS, COLS), COLS)

    def x_copy(k, p):
        return pltpu.make_async_remote_copy(
            xsend.at[k, p], part.at[k, p], x_send_sem.at[k, p], x_recv_sem.at[k, p],
            device_id=sibling, device_id_type=MESH)

    def wide_copy(n, way):
        k, count = (BEHIND, AHEAD)[way], (LAST, LAST, 1)[n]
        first = ((HALF, 1), (0, HALF + 1), (LAST, HALF))[n][way]
        return pltpu.make_async_remote_copy(
            part.at[k, pl.ds(first, count)], (yb, yc, yc)[n].at[way, pl.ds(first % HALF, count)],
            w_send_sem.at[n, way], w_recv_sem.at[n, way],
            device_id=y_peer((BEHIND, AHEAD)[way]), device_id_type=MESH)

    def x_half(k, half):
        pieces = pl.ds(half * HALF, HALF)
        return pltpu.make_async_remote_copy(
            xsend.at[k, pieces], part.at[k, pieces], x_send_sem.at[k, half], x_recv_sem.at[k, half],
            device_id=sibling, device_id_type=MESH)

    def widen(k, p):
        xsend[k, p] = raw_v[k, 1, :, columns(p)].astype(F32)

    def tell(sem, peer):
        pl.semaphore_signal(sem, inc=1, device_id=peer, device_id_type=MESH)

    @pl.when(core == 1)
    def _():
        @pl.when(odd)
        def _():
            pl.semaphore_wait(barrier, 5)
            for step in (AHEAD, BEHIND):
                for of in range(CORES):
                    tell(near_sem, y_peer(step, of))

        @pl.when(jnp.logical_not(odd))
        def _():
            pl.semaphore_wait(barrier, 1)

        tell(go_sem, sibling)

    @pl.when(core == 0)
    def _():
        pl.semaphore_wait(go_sem, 1)

    raw_copy(ACROSS, 1).wait()

    @pl.loop(0, HALF)
    def _(i):
        for p in (i, PIECES - 1 - i):
            widen(ACROSS, p)
            x_copy(ACROSS, p).start()

    for k in order[1:]:
        raw_copy(k, 1).start()
        raw_copy(k, 0).start()
    mom_copy.start()

    pos_copy.wait()
    found = pos_v[...].astype(F32).T
    for m in range(TILES):
        places[0, m] = jnp.concatenate(
            [found[8 * (4 * m + j):8 * (4 * m + j) + 8] for j in range(4)], axis=1)

    def p_copy(way):
        return pltpu.make_async_remote_copy(
            places.at[0], places.at[1 + way], p_send_sem.at[way], p_recv_sem.at[way],
            device_id=y_peer((AHEAD, BEHIND)[way]), device_id_type=MESH)

    @pl.when(jnp.logical_not(odd))
    def _():
        pl.semaphore_wait(near_sem, 2)

    for way in range(2):
        p_copy(way).start()

    def place_of(stage, way, i):
        return i if way == stage else LAST - i

    def y_copy(stage, way, i, src):
        dst = (ya, yb)[stage]
        return pltpu.make_async_remote_copy(
            src, dst.at[way, place_of(stage, way, i)], y_send_sem.at[stage, way, i], y_recv_sem.at[stage, way, i],
            device_id=y_peer((BEHIND, AHEAD)[way]), device_id_type=MESH)

    def add_sibling(k, p):
        part[k, p] = part[k, p] + raw_v[k, 0, :, columns(p)].astype(F32)

    def source(stage, way, i):
        low, high = i, PIECES - 1 - i
        if stage == 0:
            return ACROSS, (low, high)[way]
        if stage == 1:
            return (BEHIND, AHEAD)[way], (high, low)[way]
        return (BEHIND, AHEAD)[way], (low, high)[way]

    def prepare(who, p, transposed):
        place = unpack(places[who, p // 4], p).astype(jnp.int32)
        column = lanes((ROWS, BLOCK))
        pick_row = jnp.where(column == lax.shift_right_logical(place, 6), 1.0, 0.0)
        pick_col = jnp.where(column == lax.bitwise_and(place, 63), 1.0, 0.0)
        rows = jnp.dot(pick_row.astype(BF16), cos_v[...], preferred_element_type=F32)
        cols = jnp.dot(pick_col.astype(BF16), cos_v[...], preferred_element_type=F32)
        lane = lanes((ROWS, 128))
        turned = pltpu.roll(rows, 64, 1)
        left[who, p, :, 0:128] = jnp.where(lane < 64, rows, turned).astype(BF16)
        left[who, p, :, 128:256] = jnp.where(lane < 64, turned, rows).astype(BF16)
        odd = lax.rem(lax.broadcasted_iota(jnp.int32, (ROWS, 128), 0) // KEEP, 2)
        both = cols + pltpu.roll(cols, 64, 1)
        right[who, p] = jnp.where(lane // 64 == odd, both, 0.0)
        if transposed:
            for q in range(SPANS // 2):
                flat = rows[64 * q:64 * q + 64].T
                high, low = flat[0:64].astype(BF16), flat[64:128].astype(BF16)
                left_t[p, q] = jnp.concatenate([high, high, low, low], axis=1)

    def coefficients(field, who, p):
        found = []
        for h in range(2):
            high, low = split(field[:, 256 * h:256 * h + 256])
            spread = jnp.concatenate([high, low, high, low], axis=0)
            t = jnp.dot(left[who, p, 128 * h:128 * h + 128, :], spread, preferred_element_type=F32)
            t = jnp.concatenate([t[0:64, 0:128], t[64:128, 128:256]], axis=0)
            found.append(jnp.sum(t * right[who, p, 128 * h:128 * h + 128, :], axis=1, keepdims=True))
        return jnp.concatenate(found, axis=0)

    raw_copy(ACROSS, 0).wait()

    shared = jnp.where(y == 1, LAST, HALF)
    halves = (pl.ds(0, COLS // 2), pl.ds(COLS // 2, COLS // 2))
    halving = jnp.logical_and(core == 0, lax.rem(y, 2) == 1)
    halved = jnp.logical_and(core == 0, lax.rem(y, 2) == 0)

    def h_copy(way):
        return pltpu.make_async_remote_copy(
            part.at[ACROSS, shared, :, halves[way]], yh.at[way], h_send_sem.at[way], h_recv_sem.at[way],
            device_id=y_peer((BEHIND, AHEAD)[way]), device_id_type=MESH)

    def whole(way):
        return jnp.logical_not(jnp.logical_and(core == 0, y == (1, 3)[way]))

    @pl.loop(0, LAST)
    def _(i):
        for way in range(2):
            k, p = source(0, way, i)
            x_copy(k, p).wait_recv()
            add_sibling(k, p)
            y_copy(0, way, i, part.at[k, p]).start()

    for way in range(2):
        x_copy(*source(0, way, LAST)).wait_recv()
        add_sibling(*source(0, way, LAST))

    for way in range(2):
        @pl.when(whole(way))
        def _():
            y_copy(0, way, LAST, part.at[source(0, way, LAST)]).start()

    @pl.when(halving)
    def _():
        for way in range(2):
            h_copy(way).start()

    for k in order[1:]:
        raw_copy(k, 1).wait()
        for half in (1, 0) if k == BEHIND else (0, 1):
            @pl.loop(half * HALF, half * HALF + HALF)
            def _(p):
                widen(k, p)

            x_half(k, half).start()

    @pl.when(core == 0)
    def _():
        for step in range(1, X):
            greet(x_peer(step))
        for step in range(1, Z):
            greet(z_peer(step))

    for k in order[1:]:
        raw_copy(k, 0).wait()

    x_half(BEHIND, 1).wait_recv()
    x_half(AHEAD, 0).wait_recv()

    @pl.loop(0, EARLY)
    def _(i):
        for way in range(2):
            k, p = source(1, way, i)
            add_sibling(k, p)
            y_copy(1, way, i, part.at[k, p]).start()

    cos_v[...] = dct_table()
    for way in range(2):
        p_copy(way).wait_recv()

    for who in (1, 2):
        @pl.loop(0, PIECES, unroll=4)
        def _(p):
            prepare(who, p, False)

    @pl.loop(EARLY, HALF)
    def _(i):
        for way in range(2):
            add_sibling(*source(1, way, i))

    csend[...] = jnp.zeros((2, TILES, 8, 128), F32)

    def add_coefficients(way, k, p):
        csend[way, p // 4] += pack(coefficients(part[k, p], (1, 2)[way], p), p)

    joined = jnp.logical_and(core == 0, y == 2)

    @pl.loop(0, LAST + jnp.where(joined, 0, 1))
    def _(i):
        for way in range(2):
            add_coefficients(way, *source(1, way, i))

    x_half(BEHIND, 0).wait_recv()
    x_half(AHEAD, 1).wait_recv()

    @pl.loop(0, HALF)
    def _(i):
        for way in range(2):
            add_sibling(*source(2, way, i))

    mom_copy.wait()
    for half in range(2):
        x_half(0, half).wait_recv()

    @pl.loop(0, PIECES)
    def _(p):
        summed = part[0, p] + raw_v[0, 0, :, columns(p)].astype(F32)
        base[p] = 0.999 * mom_v[:, columns(p)] + summed * 0.125

    @pl.loop(0, PIECES, unroll=2)
    def _(p):
        prepare(0, p, True)

    def relay(way, i):
        k, p = source(2, way, i)
        y_copy(0, way, i, ya.at[way, i]).wait_recv()
        part[k, p] = part[k, p] + ya[way, place_of(0, way, i)]

    @pl.loop(0, LAST)
    def _(i):
        for way in range(2):
            relay(way, i)
        for way in range(2):
            add_coefficients(way, *source(2, way, i))

    @pl.when(jnp.logical_not(jnp.logical_and(core == 0, y == 0)))
    def _():
        for way in range(2):
            relay(way, LAST)

    @pl.when(halved)
    def _():
        for way in range(2):
            k, p = (BEHIND, AHEAD)[way], jnp.where(y == (0, 2)[way], LAST, HALF)
            h_copy(way).wait_recv()
            part[k, p, :, halves[way]] = part[k, p, :, halves[way]] + yh[way]

    for way in range(2):
        add_coefficients(way, *source(2, way, LAST))

    @pl.when(joined)
    def _():
        for way in range(2):
            add_coefficients(way, *source(1, way, LAST))

    def c_copy(way):
        return pltpu.make_async_remote_copy(
            csend.at[way], crecv.at[way], c_send_sem.at[way], c_recv_sem.at[way],
            device_id=y_peer((BEHIND, AHEAD)[way]), device_id_type=MESH)

    for way in range(2):
        c_copy(way).start()

    def send_rest():
        for n in range(3):
            for way in range(2):
                wide_copy(n, way).start()

    pl.when(core == 1)(send_rest)

    xslots[x, core] = jnp.zeros((TILES, 8, 128), F32)

    @pl.loop(0, PIECES, unroll=2)
    def _(p):
        xslots[x, core, p // 4] += pack(coefficients(base[p], 0, p), p)

    for way in range(2):
        c_copy(way).wait_recv()
    xslots[x, core] = xslots[x, core] + (crecv[0] + crecv[1]) * 0.125

    def pair_copy(back):
        ref = total.at[1] if back else xslots.at[x, 1]
        return pltpu.make_async_remote_copy(
            ref, ref, pair_send_sem.at[back], pair_recv_sem.at[back],
            device_id=sibling, device_id_type=MESH)

    def rx_copy(step):
        return pltpu.make_async_remote_copy(
            xslots.at[x], xslots.at[x], rx_send_sem.at[step - 1], rx_recv_sem.at[step - 1],
            device_id=x_peer(step), device_id_type=MESH)

    def rz_copy(step):
        return pltpu.make_async_remote_copy(
            zslots.at[z], zslots.at[z], rz_send_sem.at[step - 1], rz_recv_sem.at[step - 1],
            device_id=z_peer(step), device_id_type=MESH)

    @pl.when(core == 1)
    def _():
        pair_copy(0).start()

    @pl.when(core == 0)
    def _():
        pl.semaphore_wait(barrier, X - 1 + Z - 1)
        pair_copy(0).wait_recv()
        for step in X_STEPS:
            rx_copy(step).start()

    def inverse(p, q, column):
        high, low = split(column * right[0, p, 64 * q:64 * q + 64, :])
        spread = jnp.concatenate([high, low, high, low], axis=0)
        return jnp.dot(left_t[p, q], spread, preferred_element_type=F32)

    @pl.loop(0, PIECES, unroll=4)
    def _(p):
        column = unpack(xslots[x, core, p // 4], p)
        for q in range(SPANS // 2):
            base[p, :, 128 * q:128 * q + 128] -= inverse(p, q, column[64 * q:64 * q + 64])

    @pl.when(core == 0)
    def _():
        for step in range(1, X):
            rx_copy(step).wait_recv()
        send_rest()
        zslots[z] = (xslots[0] + xslots[1]) + (xslots[2] + xslots[3])
        for step in Z_STEPS:
            rz_copy(step).start()
        for step in range(1, Z):
            rz_copy(step).wait_recv()
        summed = zslots[0]
        for s in range(1, Z):
            summed = summed + zslots[s]
        total[...] = summed
        pair_copy(1).start()

    @pl.when(core == 1)
    def _():
        pair_copy(1).wait_recv()

    @pl.loop(0, PIECES, unroll=4)
    def _(p):
        column = unpack(total[core, p // 4], p)
        mean = jnp.sum((column * column).reshape(SPANS, KEEP, 1), axis=1, keepdims=True)
        scale = 1.0 / jnp.sqrt(mean * (1.0 / (BLOCK * BLOCK)) + 1e-06)
        column = column * jnp.broadcast_to(scale, (SPANS, KEEP, 1)).reshape(ROWS, 1)
        for q in range(SPANS // 2):
            at = pl.ds(pl.multiple_of(p * COLS + 128 * q, 128), 128)
            out_u[:, at] = jnp.tanh(inverse(p, q, column[64 * q:64 * q + 64]))

    for way in range(2):
        y_copy(1, way, 0, yb.at[way, 0]).wait_recv()
        wide_copy(0, way).wait_recv()

    @pl.loop(0, HALF)
    def _(i):
        base[HALF + i] += yb[0, i] * 0.125
        base[i] += yb[1, i] * 0.125

    for way in range(2):
        p_copy(way).wait_send()
        c_copy(way).wait_send()

    @pl.when(core == 1)
    def _():
        pair_copy(0).wait_send()

    @pl.when(core == 0)
    def _():
        pair_copy(1).wait_send()
        for step in range(1, X):
            rx_copy(step).wait_send()
        for step in range(1, Z):
            rz_copy(step).wait_send()

    @pl.loop(0, PIECES)
    def _(p):
        x_copy(ACROSS, p).wait_send()

    for k in order[1:]:
        for half in range(2):
            x_half(k, half).wait_send()

    @pl.loop(0, LAST)
    def _(i):
        for way in range(2):
            y_copy(0, way, i, ya.at[way, i]).wait_send()

    for way in range(2):
        @pl.when(whole(way))
        def _():
            y_copy(0, way, LAST, ya.at[way, LAST]).wait_send()

    @pl.when(halving)
    def _():
        for way in range(2):
            h_copy(way).wait_send()

    for way in range(2):
        y_copy(1, way, 0, yb.at[way, 0]).wait_send()
        wide_copy(0, way).wait_send()

    def finish(p, way):
        out_m[0, :, columns(p)] = base[p] + yc[way, lax.rem(p, HALF)] * 0.125

    for way in range(2):
        wide_copy(1, way).wait_recv()

    @pl.loop(0, LAST)
    def _(i):
        finish(i, 0)
        finish(HALF + 1 + i, 1)

    for way in range(2):
        wide_copy(2, way).wait_recv()
        finish(jnp.int32((LAST, HALF)[way]), way)
    for n in (1, 2):
        for way in range(2):
            wide_copy(n, way).wait_send()


def write_out(new_m, new_u, out_m, out_u, sem):
    copy_m = pltpu.make_async_copy(new_m, out_m, sem.at[0])
    copy_u = pltpu.make_async_copy(new_u, out_u, sem.at[1])
    copy_m.start()
    copy_u.start()
    copy_m.wait()
    copy_u.wait()


def per_device(raw_grads, momentum, positions):
    piece = (BLOCK, COLS)
    tiles = (TILES, 8, 128)
    dma = pltpu.SemaphoreType.DMA
    shapes = ((1, BLOCK, WIDTH), (BLOCK, WIDTH))
    anywhere = pl.BlockSpec(memory_space=pl.ANY)
    inputs = (raw_grads, momentum, positions.T)
    results = pl.pallas_call(
        kernel,
        out_shape=tuple(pltpu.VMEM(shape, F32) for shape in shapes),
        in_specs=[anywhere] * 3,
        out_specs=tuple(pl.BlockSpec(memory_space=pltpu.VMEM) for _ in shapes),
        scratch_shapes=[
            pltpu.VMEM((Y, 2, BLOCK, WIDTH), BF16),
            pltpu.VMEM((BLOCK, WIDTH), F32),
            pltpu.VMEM((KEEP, WIDTH // BLOCK), jnp.int32),
            pltpu.VMEM((BLOCK, 2 * BLOCK), BF16),
            pltpu.VMEM((Y, PIECES) + piece, F32),
            pltpu.VMEM((Y, PIECES) + piece, F32),
            pltpu.VMEM((2, HALF) + piece, F32),
            pltpu.VMEM((2, BLOCK, COLS // 2), F32),
            pltpu.VMEM((2, HALF) + piece, F32),
            pltpu.VMEM((2, HALF) + piece, F32),
            pltpu.VMEM((PIECES,) + piece, F32),
            pltpu.VMEM((3,) + tiles, F32),
            pltpu.VMEM((3, PIECES, ROWS, 256), BF16),
            pltpu.VMEM((3, PIECES, ROWS, 128), F32),
            pltpu.VMEM((PIECES, SPANS // 2, BLOCK, 256), BF16),
            pltpu.VMEM((2,) + tiles, F32),
            pltpu.VMEM((2,) + tiles, F32),
            pltpu.VMEM((X, CORES) + tiles, F32),
            pltpu.VMEM((Z, CORES) + tiles, F32),
            pltpu.VMEM((CORES,) + tiles, F32),
            dma((Y, 2)), dma((2,)), pltpu.SemaphoreType.REGULAR, pltpu.SemaphoreType.REGULAR,
            dma((Y, PIECES)), dma((Y, PIECES)),
            dma((2, 2, HALF)), dma((2, 2, HALF)), dma((3, 2)), dma((3, 2)), dma((2,)), dma((2,)),
            dma((2,)), dma((2,)), dma((2,)), dma((2,)),
            dma((X - 1,)), dma((X - 1,)), dma((Z - 1,)), dma((Z - 1,)),
            dma((2,)), dma((2,)),
        ],
        compiler_params=pltpu.CompilerParams(
            collective_id=0, has_side_effects=True, vmem_limit_bytes=48 * 1024 * 1024),
    )(*(pltpu.with_memory_space_constraint(v, pltpu.HBM) for v in inputs))
    return pl.pallas_call(
        write_out,
        out_shape=tuple(pltpu.HBM(shape, F32) for shape in shapes),
        in_specs=[anywhere] * 2,
        out_specs=(anywhere, anywhere),
        scratch_shapes=[dma((2,))],
        compiler_params=pltpu.CompilerParams(vmem_limit_bytes=4 * 1024 * 1024),
    )(*(pltpu.with_memory_space_constraint(v, pltpu.VMEM) for v in results))


def solution(mesh):
    placed = (P(("rep", "fsdp"), None, None), P("rep", None, "fsdp"), P("fsdp", None))
    return jax.shard_map(
        per_device,
        mesh=mesh,
        in_specs=placed,
        out_specs=(P("rep", None, "fsdp"), P(None, "fsdp")),
        check_vma=False,
    )
```

```python
import math

import jax
import jax.numpy as jnp
from jax import lax
from jax.experimental import pallas as pl
from jax.experimental.pallas import tpu as pltpu
from jax.sharding import PartitionSpec as P

MESH = pl.DeviceIdType.MESH
F32, BF16 = jnp.float32, jnp.bfloat16

BLOCK = 64
KEEP = 32
X, Y, Z, CORES = 4, 4, 8, 2
WIDTH = 4096
PIECES = 8
HALF = PIECES // 2
LAST = HALF - 1
COLS = WIDTH // PIECES
SPANS = COLS // BLOCK
ROWS = SPANS * KEEP
TILES = PIECES * SPANS * KEEP // (8 * 128)
AHEAD, BEHIND, ACROSS = 1, 3, 2
X_STEPS, Z_STEPS = (2, 1, 3), (4, 3, 5, 2, 6, 1, 7)
EARLY = 1


def split(x):
    high = x.astype(BF16)
    return high, (x - high.astype(F32)).astype(BF16)


def dct_table():
    k = lax.broadcasted_iota(jnp.int32, (BLOCK, BLOCK), 0)
    j = lax.broadcasted_iota(jnp.int32, (BLOCK, BLOCK), 1)
    turn = lax.rem((2 * j + 1) * k, 4 * BLOCK)
    cosines = jnp.cos(turn.astype(F32) * (math.pi / (2 * BLOCK))) * math.sqrt(2.0 / BLOCK)
    high, low = split(jnp.where(k == 0, cosines * math.sqrt(0.5), cosines))
    return jnp.concatenate([high, low], axis=1)


def lanes(shape):
    return lax.broadcasted_iota(jnp.int32, shape, 1)


def own_lane(piece):
    row = lax.broadcasted_iota(jnp.int32, (ROWS, 128), 0)
    return lanes((ROWS, 128)) == lax.rem(row, KEEP) + KEEP * lax.rem(piece, 4)


def unpack(tile, piece):
    wide = jnp.broadcast_to(tile[:, None, :], (SPANS, KEEP, 128)).reshape(ROWS, 128)
    return jnp.sum(jnp.where(own_lane(piece), wide, 0.0), axis=1, keepdims=True)


def pack(column, piece):
    wide = jnp.where(own_lane(piece), column, 0.0)
    return jnp.sum(wide.reshape(SPANS, KEEP, 128), axis=1)


def kernel(
    raw, mom, pos, out_m, out_u,
    raw_v, mom_v, pos_v, cos_v, xsend, part, ya, yh, yb, yc, base,
    places, left, right, left_t, csend, crecv, xslots, zslots, total,
    raw_sem, in_sem, go_sem, near_sem, x_send_sem, x_recv_sem, y_send_sem, y_recv_sem, w_send_sem, w_recv_sem, h_send_sem, h_recv_sem,
    p_send_sem, p_recv_sem, c_send_sem, c_recv_sem,
    rx_send_sem, rx_recv_sem, rz_send_sem, rz_recv_sem, pair_send_sem, pair_recv_sem,
):
    rep, fs = lax.axis_index("rep"), lax.axis_index("fsdp")
    y, core = fs // CORES, lax.rem(fs, CORES)
    x, z = rep // Z, lax.rem(rep, Z)

    def y_peer(step, of=core):
        return (rep, lax.rem(y + step, Y) * CORES + of)

    def x_peer(step):
        return (lax.rem(x + step, X) * Z + z, fs)

    def z_peer(step):
        return (x * Z + lax.rem(z + step, Z), fs)

    sibling = (rep, y * CORES + 1 - core)

    barrier = pltpu.get_barrier_semaphore()
    odd = lax.rem(y, 2) == 1

    def greet(peer):
        pl.semaphore_signal(barrier, inc=1, device_id=peer, device_id_type=MESH)

    @pl.when(jnp.logical_not(odd))
    def _():
        greet(y_peer(AHEAD, 1))
        greet(y_peer(BEHIND, 1))

    @pl.when(core == 0)
    def _():
        greet(sibling)

    def raw_copy(k, slot):
        owner = lax.rem(y + k, Y) * CORES + (core if slot == 0 else 1 - core)
        start = pl.multiple_of(owner * WIDTH, WIDTH)
        return pltpu.make_async_copy(
            raw.at[0, :, pl.ds(start, WIDTH)], raw_v.at[k, slot], raw_sem.at[k, slot])

    order = (ACROSS, BEHIND, AHEAD, 0)
    pos_copy = pltpu.make_async_copy(pos, pos_v, in_sem.at[0])
    mom_copy = pltpu.make_async_copy(mom.at[0], mom_v, in_sem.at[1])
    raw_copy(ACROSS, 1).start()
    pos_copy.start()
    raw_copy(ACROSS, 0).start()

    def columns(piece):
        return pl.ds(pl.multiple_of(piece * COLS, COLS), COLS)

    def x_copy(k, p):
        return pltpu.make_async_remote_copy(
            xsend.at[k, p], part.at[k, p], x_send_sem.at[k, p], x_recv_sem.at[k, p],
            device_id=sibling, device_id_type=MESH)

    def wide_copy(n, way):
        k, count = (BEHIND, AHEAD)[way], (LAST, LAST, 1)[n]
        first = ((HALF, 1), (0, HALF + 1), (LAST, HALF))[n][way]
        return pltpu.make_async_remote_copy(
            part.at[k, pl.ds(first, count)], (yb, yc, yc)[n].at[way, pl.ds(first % HALF, count)],
            w_send_sem.at[n, way], w_recv_sem.at[n, way],
            device_id=y_peer((BEHIND, AHEAD)[way]), device_id_type=MESH)

    def x_half(k, half):
        pieces = pl.ds(half * HALF, HALF)
        return pltpu.make_async_remote_copy(
            xsend.at[k, pieces], part.at[k, pieces], x_send_sem.at[k, half], x_recv_sem.at[k, half],
            device_id=sibling, device_id_type=MESH)

    def widen(k, p):
        xsend[k, p] = raw_v[k, 1, :, columns(p)].astype(F32)

    def tell(sem, peer):
        pl.semaphore_signal(sem, inc=1, device_id=peer, device_id_type=MESH)

    @pl.when(core == 1)
    def _():
        @pl.when(odd)
        def _():
            pl.semaphore_wait(barrier, 5)
            for step in (AHEAD, BEHIND):
                for of in range(CORES):
                    tell(near_sem, y_peer(step, of))

        @pl.when(jnp.logical_not(odd))
        def _():
            pl.semaphore_wait(barrier, 1)

        tell(go_sem, sibling)

    @pl.when(core == 0)
    def _():
        pl.semaphore_wait(go_sem, 1)

    raw_copy(ACROSS, 1).wait()

    widen(ACROSS, 0)
    x_copy(ACROSS, 0).start()
    widen(ACROSS, PIECES - 1)
    x_copy(ACROSS, PIECES - 1).start()

    @pl.loop(1, HALF)
    def _(i):
        for p in (i, PIECES - 1 - i):
            widen(ACROSS, p)
            x_copy(ACROSS, p).start()

    for k in order[1:]:
        raw_copy(k, 1).start()
        raw_copy(k, 0).start()
    mom_copy.start()

    pos_copy.wait()
    found = pos_v[...].astype(F32).T
    for m in range(TILES):
        places[0, m] = jnp.concatenate(
            [found[8 * (4 * m + j):8 * (4 * m + j) + 8] for j in range(4)], axis=1)

    def p_copy(way):
        return pltpu.make_async_remote_copy(
            places.at[0], places.at[1 + way], p_send_sem.at[way], p_recv_sem.at[way],
            device_id=y_peer((AHEAD, BEHIND)[way]), device_id_type=MESH)

    @pl.when(jnp.logical_not(odd))
    def _():
        pl.semaphore_wait(near_sem, 2)

    for way in range(2):
        p_copy(way).start()

    def place_of(stage, way, i):
        return i if way == stage else LAST - i

    def y_copy(stage, way, i, src):
        dst = (ya, yb)[stage]
        return pltpu.make_async_remote_copy(
            src, dst.at[way, place_of(stage, way, i)], y_send_sem.at[stage, way, i], y_recv_sem.at[stage, way, i],
            device_id=y_peer((BEHIND, AHEAD)[way]), device_id_type=MESH)

    def add_sibling(k, p):
        part[k, p] = part[k, p] + raw_v[k, 0, :, columns(p)].astype(F32)

    def source(stage, way, i):
        low, high = i, PIECES - 1 - i
        if stage == 0:
            return ACROSS, (low, high)[way]
        if stage == 1:
            return (BEHIND, AHEAD)[way], (high, low)[way]
        return (BEHIND, AHEAD)[way], (low, high)[way]

    def prepare(who, p, transposed):
        place = unpack(places[who, p // 4], p).astype(jnp.int32)
        column = lanes((ROWS, BLOCK))
        pick_row = jnp.where(column == lax.shift_right_logical(place, 6), 1.0, 0.0)
        pick_col = jnp.where(column == lax.bitwise_and(place, 63), 1.0, 0.0)
        rows = jnp.dot(pick_row.astype(BF16), cos_v[...], preferred_element_type=F32)
        cols = jnp.dot(pick_col.astype(BF16), cos_v[...], preferred_element_type=F32)
        lane = lanes((ROWS, 128))
        turned = pltpu.roll(rows, 64, 1)
        left[who, p, :, 0:128] = jnp.where(lane < 64, rows, turned).astype(BF16)
        left[who, p, :, 128:256] = jnp.where(lane < 64, turned, rows).astype(BF16)
        odd = lax.rem(lax.broadcasted_iota(jnp.int32, (ROWS, 128), 0) // KEEP, 2)
        both = cols + pltpu.roll(cols, 64, 1)
        right[who, p] = jnp.where(lane // 64 == odd, both, 0.0)
        if transposed:
            for q in range(SPANS // 2):
                flat = rows[64 * q:64 * q + 64].T
                high, low = flat[0:64].astype(BF16), flat[64:128].astype(BF16)
                left_t[p, q] = jnp.concatenate([high, high, low, low], axis=1)

    def coefficients(field, who, p):
        found = []
        for h in range(2):
            high, low = split(field[:, 256 * h:256 * h + 256])
            spread = jnp.concatenate([high, low, high, low], axis=0)
            t = jnp.dot(left[who, p, 128 * h:128 * h + 128, :], spread, preferred_element_type=F32)
            t = jnp.concatenate([t[0:64, 0:128], t[64:128, 128:256]], axis=0)
            found.append(jnp.sum(t * right[who, p, 128 * h:128 * h + 128, :], axis=1, keepdims=True))
        return jnp.concatenate(found, axis=0)

    raw_copy(ACROSS, 0).wait()

    shared = jnp.where(y == 1, LAST, HALF)
    halves = (pl.ds(0, COLS // 2), pl.ds(COLS // 2, COLS // 2))
    halving = jnp.logical_and(core == 0, lax.rem(y, 2) == 1)
    halved = jnp.logical_and(core == 0, lax.rem(y, 2) == 0)

    def h_copy(way):
        return pltpu.make_async_remote_copy(
            part.at[ACROSS, shared, :, halves[way]], yh.at[way], h_send_sem.at[way], h_recv_sem.at[way],
            device_id=y_peer((BEHIND, AHEAD)[way]), device_id_type=MESH)

    def whole(way):
        return jnp.logical_not(jnp.logical_and(core == 0, y == (1, 3)[way]))

    @pl.loop(0, LAST)
    def _(i):
        for way in range(2):
            k, p = source(0, way, i)
            x_copy(k, p).wait_recv()
            add_sibling(k, p)
            y_copy(0, way, i, part.at[k, p]).start()

    for way in range(2):
        x_copy(*source(0, way, LAST)).wait_recv()
        add_sibling(*source(0, way, LAST))

    for way in range(2):
        @pl.when(whole(way))
        def _():
            y_copy(0, way, LAST, part.at[source(0, way, LAST)]).start()

    @pl.when(halving)
    def _():
        for way in range(2):
            h_copy(way).start()

    for k in order[1:]:
        raw_copy(k, 1).wait()
        for half in (1, 0) if k == BEHIND else (0, 1):
            @pl.loop(half * HALF, half * HALF + HALF)
            def _(p):
                widen(k, p)

            x_half(k, half).start()

    @pl.when(core == 0)
    def _():
        for step in range(1, X):
            greet(x_peer(step))
        for step in range(1, Z):
            greet(z_peer(step))

    for k in order[1:]:
        raw_copy(k, 0).wait()

    x_half(BEHIND, 1).wait_recv()
    x_half(AHEAD, 0).wait_recv()

    @pl.loop(0, EARLY)
    def _(i):
        for way in range(2):
            k, p = source(1, way, i)
            add_sibling(k, p)
            y_copy(1, way, i, part.at[k, p]).start()

    cos_v[...] = dct_table()
    for way in range(2):
        p_copy(way).wait_recv()

    for who in (1, 2):
        @pl.loop(0, PIECES, unroll=4)
        def _(p):
            prepare(who, p, False)

    @pl.loop(EARLY, HALF)
    def _(i):
        for way in range(2):
            add_sibling(*source(1, way, i))

    csend[...] = jnp.zeros((2, TILES, 8, 128), F32)

    def add_coefficients(way, k, p):
        csend[way, p // 4] += pack(coefficients(part[k, p], (1, 2)[way], p), p)

    joined = jnp.logical_and(core == 0, y == 2)

    @pl.loop(0, LAST + jnp.where(joined, 0, 1))
    def _(i):
        for way in range(2):
            add_coefficients(way, *source(1, way, i))

    x_half(BEHIND, 0).wait_recv()
    x_half(AHEAD, 1).wait_recv()

    @pl.loop(0, HALF)
    def _(i):
        for way in range(2):
            add_sibling(*source(2, way, i))

    mom_copy.wait()
    for half in range(2):
        x_half(0, half).wait_recv()

    @pl.loop(0, PIECES)
    def _(p):
        summed = part[0, p] + raw_v[0, 0, :, columns(p)].astype(F32)
        base[p] = 0.999 * mom_v[:, columns(p)] + summed * 0.125

    @pl.loop(0, PIECES, unroll=2)
    def _(p):
        prepare(0, p, True)

    def relay(way, i):
        k, p = source(2, way, i)
        y_copy(0, way, i, ya.at[way, i]).wait_recv()
        part[k, p] = part[k, p] + ya[way, place_of(0, way, i)]

    @pl.loop(0, LAST)
    def _(i):
        for way in range(2):
            relay(way, i)
        for way in range(2):
            add_coefficients(way, *source(2, way, i))

    @pl.when(jnp.logical_not(jnp.logical_and(core == 0, y == 0)))
    def _():
        for way in range(2):
            relay(way, LAST)

    @pl.when(halved)
    def _():
        for way in range(2):
            k, p = (BEHIND, AHEAD)[way], jnp.where(y == (0, 2)[way], LAST, HALF)
            h_copy(way).wait_recv()
            part[k, p, :, halves[way]] = part[k, p, :, halves[way]] + yh[way]

    for way in range(2):
        add_coefficients(way, *source(2, way, LAST))

    @pl.when(joined)
    def _():
        for way in range(2):
            add_coefficients(way, *source(1, way, LAST))

    def c_copy(way):
        return pltpu.make_async_remote_copy(
            csend.at[way], crecv.at[way], c_send_sem.at[way], c_recv_sem.at[way],
            device_id=y_peer((BEHIND, AHEAD)[way]), device_id_type=MESH)

    for way in range(2):
        c_copy(way).start()

    def send_rest():
        for n in range(3):
            for way in range(2):
                wide_copy(n, way).start()

    pl.when(core == 1)(send_rest)

    xslots[x, core] = jnp.zeros((TILES, 8, 128), F32)

    @pl.loop(0, PIECES, unroll=2)
    def _(p):
        xslots[x, core, p // 4] += pack(coefficients(base[p], 0, p), p)

    for way in range(2):
        c_copy(way).wait_recv()
    xslots[x, core] = xslots[x, core] + (crecv[0] + crecv[1]) * 0.125

    def pair_copy(back):
        ref = total.at[1] if back else xslots.at[x, 1]
        return pltpu.make_async_remote_copy(
            ref, ref, pair_send_sem.at[back], pair_recv_sem.at[back],
            device_id=sibling, device_id_type=MESH)

    def rx_copy(step):
        return pltpu.make_async_remote_copy(
            xslots.at[x], xslots.at[x], rx_send_sem.at[step - 1], rx_recv_sem.at[step - 1],
            device_id=x_peer(step), device_id_type=MESH)

    def rz_copy(step):
        return pltpu.make_async_remote_copy(
            zslots.at[z], zslots.at[z], rz_send_sem.at[step - 1], rz_recv_sem.at[step - 1],
            device_id=z_peer(step), device_id_type=MESH)

    @pl.when(core == 1)
    def _():
        pair_copy(0).start()

    @pl.when(core == 0)
    def _():
        pl.semaphore_wait(barrier, X - 1 + Z - 1)
        pair_copy(0).wait_recv()
        for step in X_STEPS:
            rx_copy(step).start()

    def inverse(p, q, column):
        high, low = split(column * right[0, p, 64 * q:64 * q + 64, :])
        spread = jnp.concatenate([high, low, high, low], axis=0)
        return jnp.dot(left_t[p, q], spread, preferred_element_type=F32)

    @pl.loop(0, PIECES, unroll=4)
    def _(p):
        column = unpack(xslots[x, core, p // 4], p)
        for q in range(SPANS // 2):
            base[p, :, 128 * q:128 * q + 128] -= inverse(p, q, column[64 * q:64 * q + 64])

    @pl.when(core == 0)
    def _():
        for step in range(1, X):
            rx_copy(step).wait_recv()
        send_rest()
        zslots[z] = (xslots[0] + xslots[1]) + (xslots[2] + xslots[3])
        for step in Z_STEPS:
            rz_copy(step).start()
        for step in range(1, Z):
            rz_copy(step).wait_recv()
        summed = zslots[0]
        for s in range(1, Z):
            summed = summed + zslots[s]
        total[...] = summed
        pair_copy(1).start()

    @pl.when(core == 1)
    def _():
        pair_copy(1).wait_recv()

    @pl.loop(0, PIECES, unroll=4)
    def _(p):
        column = unpack(total[core, p // 4], p)
        mean = jnp.sum((column * column).reshape(SPANS, KEEP, 1), axis=1, keepdims=True)
        scale = 1.0 / jnp.sqrt(mean * (1.0 / (BLOCK * BLOCK)) + 1e-06)
        column = column * jnp.broadcast_to(scale, (SPANS, KEEP, 1)).reshape(ROWS, 1)
        for q in range(SPANS // 2):
            at = pl.ds(pl.multiple_of(p * COLS + 128 * q, 128), 128)
            out_u[:, at] = jnp.tanh(inverse(p, q, column[64 * q:64 * q + 64]))

    for way in range(2):
        y_copy(1, way, 0, yb.at[way, 0]).wait_recv()
        wide_copy(0, way).wait_recv()

    @pl.loop(0, HALF)
    def _(i):
        base[HALF + i] += yb[0, i] * 0.125
        base[i] += yb[1, i] * 0.125

    for way in range(2):
        p_copy(way).wait_send()
        c_copy(way).wait_send()

    @pl.when(core == 1)
    def _():
        pair_copy(0).wait_send()

    @pl.when(core == 0)
    def _():
        pair_copy(1).wait_send()
        for step in range(1, X):
            rx_copy(step).wait_send()
        for step in range(1, Z):
            rz_copy(step).wait_send()

    @pl.loop(0, PIECES)
    def _(p):
        x_copy(ACROSS, p).wait_send()

    for k in order[1:]:
        for half in range(2):
            x_half(k, half).wait_send()

    @pl.loop(0, LAST)
    def _(i):
        for way in range(2):
            y_copy(0, way, i, ya.at[way, i]).wait_send()

    for way in range(2):
        @pl.when(whole(way))
        def _():
            y_copy(0, way, LAST, ya.at[way, LAST]).wait_send()

    @pl.when(halving)
    def _():
        for way in range(2):
            h_copy(way).wait_send()

    for way in range(2):
        y_copy(1, way, 0, yb.at[way, 0]).wait_send()
        wide_copy(0, way).wait_send()

    def finish(p, way):
        out_m[0, :, columns(p)] = base[p] + yc[way, lax.rem(p, HALF)] * 0.125

    for way in range(2):
        wide_copy(1, way).wait_recv()

    @pl.loop(0, LAST)
    def _(i):
        finish(i, 0)
        finish(HALF + 1 + i, 1)

    for way in range(2):
        wide_copy(2, way).wait_recv()
        finish(jnp.int32((LAST, HALF)[way]), way)
    for n in (1, 2):
        for way in range(2):
            wide_copy(n, way).wait_send()


def write_out(new_m, new_u, out_m, out_u, sem):
    copy_m = pltpu.make_async_copy(new_m, out_m, sem.at[0])
    copy_u = pltpu.make_async_copy(new_u, out_u, sem.at[1])
    copy_m.start()
    copy_u.start()
    copy_m.wait()
    copy_u.wait()


def per_device(raw_grads, momentum, positions):
    piece = (BLOCK, COLS)
    tiles = (TILES, 8, 128)
    dma = pltpu.SemaphoreType.DMA
    shapes = ((1, BLOCK, WIDTH), (BLOCK, WIDTH))
    anywhere = pl.BlockSpec(memory_space=pl.ANY)
    inputs = (raw_grads, momentum, positions.T)
    results = pl.pallas_call(
        kernel,
        out_shape=tuple(pltpu.VMEM(shape, F32) for shape in shapes),
        in_specs=[anywhere] * 3,
        out_specs=tuple(pl.BlockSpec(memory_space=pltpu.VMEM) for _ in shapes),
        scratch_shapes=[
            pltpu.VMEM((Y, 2, BLOCK, WIDTH), BF16),
            pltpu.VMEM((BLOCK, WIDTH), F32),
            pltpu.VMEM((KEEP, WIDTH // BLOCK), jnp.int32),
            pltpu.VMEM((BLOCK, 2 * BLOCK), BF16),
            pltpu.VMEM((Y, PIECES) + piece, F32),
            pltpu.VMEM((Y, PIECES) + piece, F32),
            pltpu.VMEM((2, HALF) + piece, F32),
            pltpu.VMEM((2, BLOCK, COLS // 2), F32),
            pltpu.VMEM((2, HALF) + piece, F32),
            pltpu.VMEM((2, HALF) + piece, F32),
            pltpu.VMEM((PIECES,) + piece, F32),
            pltpu.VMEM((3,) + tiles, F32),
            pltpu.VMEM((3, PIECES, ROWS, 256), BF16),
            pltpu.VMEM((3, PIECES, ROWS, 128), F32),
            pltpu.VMEM((PIECES, SPANS // 2, BLOCK, 256), BF16),
            pltpu.VMEM((2,) + tiles, F32),
            pltpu.VMEM((2,) + tiles, F32),
            pltpu.VMEM((X, CORES) + tiles, F32),
            pltpu.VMEM((Z, CORES) + tiles, F32),
            pltpu.VMEM((CORES,) + tiles, F32),
            dma((Y, 2)), dma((2,)), pltpu.SemaphoreType.REGULAR, pltpu.SemaphoreType.REGULAR,
            dma((Y, PIECES)), dma((Y, PIECES)),
            dma((2, 2, HALF)), dma((2, 2, HALF)), dma((3, 2)), dma((3, 2)), dma((2,)), dma((2,)),
            dma((2,)), dma((2,)), dma((2,)), dma((2,)),
            dma((X - 1,)), dma((X - 1,)), dma((Z - 1,)), dma((Z - 1,)),
            dma((2,)), dma((2,)),
        ],
        compiler_params=pltpu.CompilerParams(
            collective_id=0, has_side_effects=True, vmem_limit_bytes=48 * 1024 * 1024),
    )(*(pltpu.with_memory_space_constraint(v, pltpu.HBM) for v in inputs))
    return pl.pallas_call(
        write_out,
        out_shape=tuple(pltpu.HBM(shape, F32) for shape in shapes),
        in_specs=[anywhere] * 2,
        out_specs=(anywhere, anywhere),
        scratch_shapes=[dma((2,))],
        compiler_params=pltpu.CompilerParams(vmem_limit_bytes=4 * 1024 * 1024),
    )(*(pltpu.with_memory_space_constraint(v, pltpu.VMEM) for v in results))


def solution(mesh):
    placed = (P(("rep", "fsdp"), None, None), P("rep", None, "fsdp"), P("fsdp", None))
    return jax.shard_map(
        per_device,
        mesh=mesh,
        in_specs=placed,
        out_specs=(P("rep", None, "fsdp"), P(None, "fsdp")),
        check_vma=False,
    )
```

```python
import math

import jax
import jax.numpy as jnp
from jax import lax
from jax.experimental import pallas as pl
from jax.experimental.pallas import tpu as pltpu
from jax.sharding import PartitionSpec as P

MESH = pl.DeviceIdType.MESH
F32, BF16 = jnp.float32, jnp.bfloat16

BLOCK = 64
KEEP = 32
X, Y, Z, CORES = 4, 4, 8, 2
WIDTH = 4096
PIECES = 8
HALF = PIECES // 2
LAST = HALF - 1
COLS = WIDTH // PIECES
SPANS = COLS // BLOCK
ROWS = SPANS * KEEP
TILES = PIECES * SPANS * KEEP // (8 * 128)
AHEAD, BEHIND, ACROSS = 1, 3, 2
X_STEPS, Z_STEPS = (2, 1, 3), (4, 3, 5, 2, 6, 1, 7)
EARLY = 1


def split(x):
    high = x.astype(BF16)
    return high, (x - high.astype(F32)).astype(BF16)


def dct_table():
    k = lax.broadcasted_iota(jnp.int32, (BLOCK, BLOCK), 0)
    j = lax.broadcasted_iota(jnp.int32, (BLOCK, BLOCK), 1)
    turn = lax.rem((2 * j + 1) * k, 4 * BLOCK)
    cosines = jnp.cos(turn.astype(F32) * (math.pi / (2 * BLOCK))) * math.sqrt(2.0 / BLOCK)
    high, low = split(jnp.where(k == 0, cosines * math.sqrt(0.5), cosines))
    return jnp.concatenate([high, low], axis=1)


def lanes(shape):
    return lax.broadcasted_iota(jnp.int32, shape, 1)


def own_lane(piece):
    row = lax.broadcasted_iota(jnp.int32, (ROWS, 128), 0)
    return lanes((ROWS, 128)) == lax.rem(row, KEEP) + KEEP * lax.rem(piece, 4)


def unpack(tile, piece):
    wide = jnp.broadcast_to(tile[:, None, :], (SPANS, KEEP, 128)).reshape(ROWS, 128)
    return jnp.sum(jnp.where(own_lane(piece), wide, 0.0), axis=1, keepdims=True)


def pack(column, piece):
    wide = jnp.where(own_lane(piece), column, 0.0)
    return jnp.sum(wide.reshape(SPANS, KEEP, 128), axis=1)


def kernel(
    raw, mom, pos, out_m, out_u,
    raw_v, mom_v, pos_v, cos_v, xsend, part, ya, yh, yb, yc, base,
    places, left, right, left_t, csend, crecv, xslots, zslots, total,
    raw_sem, in_sem, go_sem, near_sem, x_send_sem, x_recv_sem, y_send_sem, y_recv_sem, w_send_sem, w_recv_sem, h_send_sem, h_recv_sem,
    p_send_sem, p_recv_sem, c_send_sem, c_recv_sem,
    rx_send_sem, rx_recv_sem, rz_send_sem, rz_recv_sem, pair_send_sem, pair_recv_sem,
):
    rep, fs = lax.axis_index("rep"), lax.axis_index("fsdp")
    y, core = fs // CORES, lax.rem(fs, CORES)
    x, z = rep // Z, lax.rem(rep, Z)

    def y_peer(step, of=core):
        return (rep, lax.rem(y + step, Y) * CORES + of)

    def x_peer(step):
        return (lax.rem(x + step, X) * Z + z, fs)

    def z_peer(step):
        return (x * Z + lax.rem(z + step, Z), fs)

    sibling = (rep, y * CORES + 1 - core)

    barrier = pltpu.get_barrier_semaphore()
    odd = lax.rem(y, 2) == 1

    def greet(peer):
        pl.semaphore_signal(barrier, inc=1, device_id=peer, device_id_type=MESH)

    @pl.when(jnp.logical_not(odd))
    def _():
        greet(y_peer(AHEAD, 1))
        greet(y_peer(BEHIND, 1))

    @pl.when(core == 0)
    def _():
        greet(sibling)

    def raw_copy(k, slot):
        owner = lax.rem(y + k, Y) * CORES + (core if slot == 0 else 1 - core)
        start = pl.multiple_of(owner * WIDTH, WIDTH)
        return pltpu.make_async_copy(
            raw.at[0, :, pl.ds(start, WIDTH)], raw_v.at[k, slot], raw_sem.at[k, slot])

    order = (ACROSS, BEHIND, AHEAD, 0)
    pos_copy = pltpu.make_async_copy(pos, pos_v, in_sem.at[0])
    mom_copy = pltpu.make_async_copy(mom.at[0], mom_v, in_sem.at[1])
    raw_copy(ACROSS, 1).start()
    pos_copy.start()
    raw_copy(ACROSS, 0).start()

    def columns(piece):
        return pl.ds(pl.multiple_of(piece * COLS, COLS), COLS)

    def x_copy(k, p):
        return pltpu.make_async_remote_copy(
            xsend.at[k, p], part.at[k, p], x_send_sem.at[k, p], x_recv_sem.at[k, p],
            device_id=sibling, device_id_type=MESH)

    def wide_copy(n, way):
        k, count = (BEHIND, AHEAD)[way], (LAST, LAST, 1)[n]
        first = ((HALF, 1), (0, HALF + 1), (LAST, HALF))[n][way]
        return pltpu.make_async_remote_copy(
            part.at[k, pl.ds(first, count)], (yb, yc, yc)[n].at[way, pl.ds(first % HALF, count)],
            w_send_sem.at[n, way], w_recv_sem.at[n, way],
            device_id=y_peer((BEHIND, AHEAD)[way]), device_id_type=MESH)

    def x_half(k, half):
        pieces = pl.ds(half * HALF, HALF)
        return pltpu.make_async_remote_copy(
            xsend.at[k, pieces], part.at[k, pieces], x_send_sem.at[k, half], x_recv_sem.at[k, half],
            device_id=sibling, device_id_type=MESH)

    def widen(k, p):
        xsend[k, p] = raw_v[k, 1, :, columns(p)].astype(F32)

    def tell(sem, peer):
        pl.semaphore_signal(sem, inc=1, device_id=peer, device_id_type=MESH)

    @pl.when(core == 1)
    def _():
        @pl.when(odd)
        def _():
            pl.semaphore_wait(barrier, 5)
            for step in (AHEAD, BEHIND):
                for of in range(CORES):
                    tell(near_sem, y_peer(step, of))

        @pl.when(jnp.logical_not(odd))
        def _():
            pl.semaphore_wait(barrier, 1)

        tell(go_sem, sibling)

    @pl.when(core == 0)
    def _():
        pl.semaphore_wait(go_sem, 1)

    raw_copy(ACROSS, 1).wait()

    widen(ACROSS, 0)
    x_copy(ACROSS, 0).start()
    widen(ACROSS, PIECES - 1)
    x_copy(ACROSS, PIECES - 1).start()

    @pl.loop(1, HALF)
    def _(i):
        for p in (i, PIECES - 1 - i):
            widen(ACROSS, p)
            x_copy(ACROSS, p).start()

    for k in order[1:]:
        raw_copy(k, 1).start()
        raw_copy(k, 0).start()
    mom_copy.start()

    pos_copy.wait()
    found = pos_v[...].astype(F32).T
    for m in range(TILES):
        places[0, m] = jnp.concatenate(
            [found[8 * (4 * m + j):8 * (4 * m + j) + 8] for j in range(4)], axis=1)

    def p_copy(way):
        return pltpu.make_async_remote_copy(
            places.at[0], places.at[1 + way], p_send_sem.at[way], p_recv_sem.at[way],
            device_id=y_peer((AHEAD, BEHIND)[way]), device_id_type=MESH)

    @pl.when(jnp.logical_not(odd))
    def _():
        pl.semaphore_wait(near_sem, 2)

    for way in range(2):
        p_copy(way).start()

    def place_of(stage, way, i):
        return i if way == stage else LAST - i

    def y_copy(stage, way, i, src):
        dst = (ya, yb)[stage]
        return pltpu.make_async_remote_copy(
            src, dst.at[way, place_of(stage, way, i)], y_send_sem.at[stage, way, i], y_recv_sem.at[stage, way, i],
            device_id=y_peer((BEHIND, AHEAD)[way]), device_id_type=MESH)

    def add_sibling(k, p):
        part[k, p] = part[k, p] + raw_v[k, 0, :, columns(p)].astype(F32)

    def source(stage, way, i):
        low, high = i, PIECES - 1 - i
        if stage == 0:
            return ACROSS, (low, high)[way]
        if stage == 1:
            return (BEHIND, AHEAD)[way], (high, low)[way]
        return (BEHIND, AHEAD)[way], (low, high)[way]

    def prepare(who, p, transposed):
        place = unpack(places[who, p // 4], p).astype(jnp.int32)
        column = lanes((ROWS, BLOCK))
        pick_row = jnp.where(column == lax.shift_right_logical(place, 6), 1.0, 0.0)
        pick_col = jnp.where(column == lax.bitwise_and(place, 63), 1.0, 0.0)
        rows = jnp.dot(pick_row.astype(BF16), cos_v[...], preferred_element_type=F32)
        cols = jnp.dot(pick_col.astype(BF16), cos_v[...], preferred_element_type=F32)
        lane = lanes((ROWS, 128))
        turned = pltpu.roll(rows, 64, 1)
        left[who, p, :, 0:128] = jnp.where(lane < 64, rows, turned).astype(BF16)
        left[who, p, :, 128:256] = jnp.where(lane < 64, turned, rows).astype(BF16)
        odd = lax.rem(lax.broadcasted_iota(jnp.int32, (ROWS, 128), 0) // KEEP, 2)
        both = cols + pltpu.roll(cols, 64, 1)
        right[who, p] = jnp.where(lane // 64 == odd, both, 0.0)
        if transposed:
            for q in range(SPANS // 2):
                flat = rows[64 * q:64 * q + 64].T
                high, low = flat[0:64].astype(BF16), flat[64:128].astype(BF16)
                left_t[p, q] = jnp.concatenate([high, high, low, low], axis=1)

    def coefficients(field, who, p):
        found = []
        for h in range(2):
            high, low = split(field[:, 256 * h:256 * h + 256])
            spread = jnp.concatenate([high, low, high, low], axis=0)
            t = jnp.dot(left[who, p, 128 * h:128 * h + 128, :], spread, preferred_element_type=F32)
            t = jnp.concatenate([t[0:64, 0:128], t[64:128, 128:256]], axis=0)
            found.append(jnp.sum(t * right[who, p, 128 * h:128 * h + 128, :], axis=1, keepdims=True))
        return jnp.concatenate(found, axis=0)

    raw_copy(ACROSS, 0).wait()

    shared = jnp.where(y == 1, LAST, HALF)
    halves = (pl.ds(0, COLS // 2), pl.ds(COLS // 2, COLS // 2))
    halving = jnp.logical_and(core == 0, lax.rem(y, 2) == 1)
    halved = jnp.logical_and(core == 0, lax.rem(y, 2) == 0)

    def h_copy(way):
        return pltpu.make_async_remote_copy(
            part.at[ACROSS, shared, :, halves[way]], yh.at[way], h_send_sem.at[way], h_recv_sem.at[way],
            device_id=y_peer((BEHIND, AHEAD)[way]), device_id_type=MESH)

    def whole(way):
        return jnp.logical_not(jnp.logical_and(core == 0, y == (1, 3)[way]))

    @pl.loop(0, LAST)
    def _(i):
        for way in range(2):
            k, p = source(0, way, i)
            x_copy(k, p).wait_recv()
            add_sibling(k, p)
            y_copy(0, way, i, part.at[k, p]).start()

    for way in range(2):
        x_copy(*source(0, way, LAST)).wait_recv()
        add_sibling(*source(0, way, LAST))

    for way in range(2):
        @pl.when(whole(way))
        def _():
            y_copy(0, way, LAST, part.at[source(0, way, LAST)]).start()

    @pl.when(halving)
    def _():
        for way in range(2):
            h_copy(way).start()

    for k in order[1:]:
        raw_copy(k, 1).wait()
        for half in (1, 0) if k == BEHIND else (0, 1):
            @pl.loop(half * HALF, half * HALF + HALF)
            def _(p):
                widen(k, p)

            x_half(k, half).start()

    @pl.when(core == 0)
    def _():
        for step in range(1, X):
            greet(x_peer(step))
        for step in range(1, Z):
            greet(z_peer(step))

    for k in order[1:]:
        raw_copy(k, 0).wait()

    x_half(BEHIND, 1).wait_recv()
    x_half(AHEAD, 0).wait_recv()

    @pl.loop(0, EARLY)
    def _(i):
        for way in range(2):
            k, p = source(1, way, i)
            add_sibling(k, p)
            y_copy(1, way, i, part.at[k, p]).start()

    cos_v[...] = dct_table()
    for way in range(2):
        p_copy(way).wait_recv()

    for who in (1, 2):
        @pl.loop(0, PIECES, unroll=4)
        def _(p):
            prepare(who, p, False)

    @pl.loop(EARLY, HALF)
    def _(i):
        for way in range(2):
            add_sibling(*source(1, way, i))

    csend[...] = jnp.zeros((2, TILES, 8, 128), F32)

    def add_coefficients(way, k, p):
        csend[way, p // 4] += pack(coefficients(part[k, p], (1, 2)[way], p), p)

    joined = jnp.logical_and(core == 0, y == 2)

    @pl.loop(0, LAST + jnp.where(joined, 0, 1))
    def _(i):
        for way in range(2):
            add_coefficients(way, *source(1, way, i))

    x_half(BEHIND, 0).wait_recv()
    x_half(AHEAD, 1).wait_recv()

    @pl.loop(0, HALF)
    def _(i):
        for way in range(2):
            add_sibling(*source(2, way, i))

    mom_copy.wait()
    for half in range(2):
        x_half(0, half).wait_recv()

    @pl.loop(0, PIECES)
    def _(p):
        summed = part[0, p] + raw_v[0, 0, :, columns(p)].astype(F32)
        base[p] = 0.999 * mom_v[:, columns(p)] + summed * 0.125

    @pl.loop(0, PIECES, unroll=2)
    def _(p):
        prepare(0, p, True)

    def relay(way, i):
        k, p = source(2, way, i)
        y_copy(0, way, i, ya.at[way, i]).wait_recv()
        part[k, p] = part[k, p] + ya[way, place_of(0, way, i)]

    @pl.loop(0, LAST)
    def _(i):
        for way in range(2):
            relay(way, i)
        for way in range(2):
            add_coefficients(way, *source(2, way, i))

    @pl.when(jnp.logical_not(jnp.logical_and(core == 0, y == 0)))
    def _():
        for way in range(2):
            relay(way, LAST)

    @pl.when(halved)
    def _():
        for way in range(2):
            k, p = (BEHIND, AHEAD)[way], jnp.where(y == (0, 2)[way], LAST, HALF)
            h_copy(way).wait_recv()
            part[k, p, :, halves[way]] = part[k, p, :, halves[way]] + yh[way]

    for way in range(2):
        add_coefficients(way, *source(2, way, LAST))

    @pl.when(joined)
    def _():
        for way in range(2):
            add_coefficients(way, *source(1, way, LAST))

    def c_copy(way):
        return pltpu.make_async_remote_copy(
            csend.at[way], crecv.at[way], c_send_sem.at[way], c_recv_sem.at[way],
            device_id=y_peer((BEHIND, AHEAD)[way]), device_id_type=MESH)

    for way in range(2):
        c_copy(way).start()

    def send_rest():
        for n in range(3):
            for way in range(2):
                wide_copy(n, way).start()

    pl.when(core == 1)(send_rest)

    xslots[x, core] = jnp.zeros((TILES, 8, 128), F32)

    @pl.loop(0, PIECES, unroll=2)
    def _(p):
        xslots[x, core, p // 4] += pack(coefficients(base[p], 0, p), p)

    for way in range(2):
        c_copy(way).wait_recv()
    xslots[x, core] = xslots[x, core] + (crecv[0] + crecv[1]) * 0.125

    def pair_copy(back):
        ref = total.at[1] if back else xslots.at[x, 1]
        return pltpu.make_async_remote_copy(
            ref, ref, pair_send_sem.at[back], pair_recv_sem.at[back],
            device_id=sibling, device_id_type=MESH)

    def rx_copy(step):
        return pltpu.make_async_remote_copy(
            xslots.at[x], xslots.at[x], rx_send_sem.at[step - 1], rx_recv_sem.at[step - 1],
            device_id=x_peer(step), device_id_type=MESH)

    def rz_copy(step):
        return pltpu.make_async_remote_copy(
            zslots.at[z], zslots.at[z], rz_send_sem.at[step - 1], rz_recv_sem.at[step - 1],
            device_id=z_peer(step), device_id_type=MESH)

    @pl.when(core == 1)
    def _():
        pair_copy(0).start()

    @pl.when(core == 0)
    def _():
        pl.semaphore_wait(barrier, X - 1 + Z - 1)
        pair_copy(0).wait_recv()
        for step in X_STEPS:
            rx_copy(step).start()
        send_rest()

    def inverse(p, q, column):
        high, low = split(column * right[0, p, 64 * q:64 * q + 64, :])
        spread = jnp.concatenate([high, low, high, low], axis=0)
        return jnp.dot(left_t[p, q], spread, preferred_element_type=F32)

    @pl.loop(0, PIECES, unroll=4)
    def _(p):
        column = unpack(xslots[x, core, p // 4], p)
        for q in range(SPANS // 2):
            base[p, :, 128 * q:128 * q + 128] -= inverse(p, q, column[64 * q:64 * q + 64])

    @pl.when(core == 0)
    def _():
        for step in range(1, X):
            rx_copy(step).wait_recv()
        zslots[z] = (xslots[0] + xslots[1]) + (xslots[2] + xslots[3])
        for step in Z_STEPS:
            rz_copy(step).start()
        for step in range(1, Z):
            rz_copy(step).wait_recv()
        summed = zslots[0]
        for s in range(1, Z):
            summed = summed + zslots[s]
        total[...] = summed
        pair_copy(1).start()

    @pl.when(core == 1)
    def _():
        pair_copy(1).wait_recv()

    @pl.loop(0, PIECES, unroll=4)
    def _(p):
        column = unpack(total[core, p // 4], p)
        mean = jnp.sum((column * column).reshape(SPANS, KEEP, 1), axis=1, keepdims=True)
        scale = 1.0 / jnp.sqrt(mean * (1.0 / (BLOCK * BLOCK)) + 1e-06)
        column = column * jnp.broadcast_to(scale, (SPANS, KEEP, 1)).reshape(ROWS, 1)
        for q in range(SPANS // 2):
            at = pl.ds(pl.multiple_of(p * COLS + 128 * q, 128), 128)
            out_u[:, at] = jnp.tanh(inverse(p, q, column[64 * q:64 * q + 64]))

    for way in range(2):
        y_copy(1, way, 0, yb.at[way, 0]).wait_recv()
        wide_copy(0, way).wait_recv()

    @pl.loop(0, HALF)
    def _(i):
        base[HALF + i] += yb[0, i] * 0.125
        base[i] += yb[1, i] * 0.125

    for way in range(2):
        p_copy(way).wait_send()
        c_copy(way).wait_send()

    @pl.when(core == 1)
    def _():
        pair_copy(0).wait_send()

    @pl.when(core == 0)
    def _():
        pair_copy(1).wait_send()
        for step in range(1, X):
            rx_copy(step).wait_send()
        for step in range(1, Z):
            rz_copy(step).wait_send()

    @pl.loop(0, PIECES)
    def _(p):
        x_copy(ACROSS, p).wait_send()

    for k in order[1:]:
        for half in range(2):
            x_half(k, half).wait_send()

    @pl.loop(0, LAST)
    def _(i):
        for way in range(2):
            y_copy(0, way, i, ya.at[way, i]).wait_send()

    for way in range(2):
        @pl.when(whole(way))
        def _():
            y_copy(0, way, LAST, ya.at[way, LAST]).wait_send()

    @pl.when(halving)
    def _():
        for way in range(2):
            h_copy(way).wait_send()

    for way in range(2):
        y_copy(1, way, 0, yb.at[way, 0]).wait_send()
        wide_copy(0, way).wait_send()

    def finish(p, way):
        out_m[0, :, columns(p)] = base[p] + yc[way, lax.rem(p, HALF)] * 0.125

    for way in range(2):
        wide_copy(1, way).wait_recv()

    @pl.loop(0, LAST)
    def _(i):
        finish(i, 0)
        finish(HALF + 1 + i, 1)

    for way in range(2):
        wide_copy(2, way).wait_recv()
        finish(jnp.int32((LAST, HALF)[way]), way)
    for n in (1, 2):
        for way in range(2):
            wide_copy(n, way).wait_send()


def write_out(new_m, new_u, out_m, out_u, sem):
    copy_m = pltpu.make_async_copy(new_m, out_m, sem.at[0])
    copy_u = pltpu.make_async_copy(new_u, out_u, sem.at[1])
    copy_m.start()
    copy_u.start()
    copy_m.wait()
    copy_u.wait()


def per_device(raw_grads, momentum, positions):
    piece = (BLOCK, COLS)
    tiles = (TILES, 8, 128)
    dma = pltpu.SemaphoreType.DMA
    shapes = ((1, BLOCK, WIDTH), (BLOCK, WIDTH))
    anywhere = pl.BlockSpec(memory_space=pl.ANY)
    inputs = (raw_grads, momentum, positions.T)
    results = pl.pallas_call(
        kernel,
        out_shape=tuple(pltpu.VMEM(shape, F32) for shape in shapes),
        in_specs=[anywhere] * 3,
        out_specs=tuple(pl.BlockSpec(memory_space=pltpu.VMEM) for _ in shapes),
        scratch_shapes=[
            pltpu.VMEM((Y, 2, BLOCK, WIDTH), BF16),
            pltpu.VMEM((BLOCK, WIDTH), F32),
            pltpu.VMEM((KEEP, WIDTH // BLOCK), jnp.int32),
            pltpu.VMEM((BLOCK, 2 * BLOCK), BF16),
            pltpu.VMEM((Y, PIECES) + piece, F32),
            pltpu.VMEM((Y, PIECES) + piece, F32),
            pltpu.VMEM((2, HALF) + piece, F32),
            pltpu.VMEM((2, BLOCK, COLS // 2), F32),
            pltpu.VMEM((2, HALF) + piece, F32),
            pltpu.VMEM((2, HALF) + piece, F32),
            pltpu.VMEM((PIECES,) + piece, F32),
            pltpu.VMEM((3,) + tiles, F32),
            pltpu.VMEM((3, PIECES, ROWS, 256), BF16),
            pltpu.VMEM((3, PIECES, ROWS, 128), F32),
            pltpu.VMEM((PIECES, SPANS // 2, BLOCK, 256), BF16),
            pltpu.VMEM((2,) + tiles, F32),
            pltpu.VMEM((2,) + tiles, F32),
            pltpu.VMEM((X, CORES) + tiles, F32),
            pltpu.VMEM((Z, CORES) + tiles, F32),
            pltpu.VMEM((CORES,) + tiles, F32),
            dma((Y, 2)), dma((2,)), pltpu.SemaphoreType.REGULAR, pltpu.SemaphoreType.REGULAR,
            dma((Y, PIECES)), dma((Y, PIECES)),
            dma((2, 2, HALF)), dma((2, 2, HALF)), dma((3, 2)), dma((3, 2)), dma((2,)), dma((2,)),
            dma((2,)), dma((2,)), dma((2,)), dma((2,)),
            dma((X - 1,)), dma((X - 1,)), dma((Z - 1,)), dma((Z - 1,)),
            dma((2,)), dma((2,)),
        ],
        compiler_params=pltpu.CompilerParams(
            collective_id=0, has_side_effects=True, vmem_limit_bytes=48 * 1024 * 1024),
    )(*(pltpu.with_memory_space_constraint(v, pltpu.HBM) for v in inputs))
    return pl.pallas_call(
        write_out,
        out_shape=tuple(pltpu.HBM(shape, F32) for shape in shapes),
        in_specs=[anywhere] * 2,
        out_specs=(anywhere, anywhere),
        scratch_shapes=[dma((2,))],
        compiler_params=pltpu.CompilerParams(vmem_limit_bytes=4 * 1024 * 1024),
    )(*(pltpu.with_memory_space_constraint(v, pltpu.VMEM) for v in results))


def solution(mesh):
    placed = (P(("rep", "fsdp"), None, None), P("rep", None, "fsdp"), P("fsdp", None))
    return jax.shard_map(
        per_device,
        mesh=mesh,
        in_specs=placed,
        out_specs=(P("rep", None, "fsdp"), P(None, "fsdp")),
        check_vma=False,
    )
```
